512 devices in a mesh: sect: 2 (over core), dp: 32 (over z_hi, y, x), tensor: 8 (over z_lo).
Axes of the slice: x: 4, y: 4, z: 16 (z_hi: 2, z_lo: 8; z = z_hi * 8 + z_lo), core: 2. Of those that a mesh axis runs over, the one named last changes fastest.
Arguments:
- teacher_rows: bfloat16 [1024, 16384], P('dp', ('sect', 'tensor')), may hold values from -48 to 48
- student_rows: bfloat16 [1024, 8192], P('dp', ('sect', 'tensor')), may hold values from -6 to 6
- projector: bfloat16 [8192, 16384], P(('sect', 'tensor'), 'dp'), may hold values from -0.0625 to 0.0625
- teacher_gain: float32 [16384], replicated, may hold values from 0.1 to 1.9
- student_gain: float32 [8192], replicated, may hold values from 0.1 to 1.9
Outputs:
- projector_grad: float32 [8192, 16384], P(('sect', 'tensor'), 'dp')
- input_grad: float32 [1024, 8192], P('dp', ('sect', 'tensor'))
The draws below stay inside these ranges and needn't reach their ends.
All inputs are finite; a program needn't handle non-finite values.
Results may differ from the reference program's by a relative error of at most 0.0048.
Values may be sent and summed in bfloat16 or wider, within the bound.
A program may use at most 64 MiB of HBM per device.

```python
import math
import jax
import jax.numpy as jnp
from jax import lax

DT = 16384
DS = 8192
TOKENS = 1024


def draw_teacher_rows(key, part):
    key = jax.random.fold_in(key, 3)
    value_key = jax.random.fold_in(key, 0)
    position = jnp.arange(DT, dtype=jnp.float32) / (DT - 1)
    column_scale = jnp.exp(jnp.log(4.0) * position)
    values = jax.random.truncated_normal(value_key, -6.0, 6.0, (TOKENS, DT), jnp.float32)
    return (values * column_scale).astype(jnp.bfloat16)


def block_scale(rng, shape, shards, least, largest):
    gain, own = 1.0, jax.random.fold_in(rng, 6)
    for axis_at, shards_of in shards:
        draws = jnp.exp(jax.random.uniform(jax.random.fold_in(own, axis_at), (shards_of,), jnp.float32, least / len(shards), largest / len(shards)))
        gain = gain * jnp.repeat(draws, shape[axis_at] // shards_of).reshape([-1 if axis == axis_at else 1 for axis in range(len(shape))])
    return gain


def centred(own_key, extent, width, most, pieces=(), kind=jnp.bfloat16):
    array = width * jax.random.normal(own_key, extent, jnp.float32)
    if pieces:
        array = array * block_scale(own_key, extent, pieces, -0.22, 0.18)
    return jnp.clip(array, -most, most).astype(kind)


def setup_inputs(seed: int = 0) -> dict:
    splits = jax.random.split(jax.random.key(seed), 6)
    teacher_rows = draw_teacher_rows(jax.random.fold_in(splits[5], 71), 0)
    student_rows = centred(splits[1], (TOKENS, DS), 1.0, 6.0, ((0, 32), (1, 16)))
    projector = centred(splits[2], (DS, DT), DS ** -0.5, 0.0625, ((0, 16), (1, 32)))
    teacher_gain = jnp.clip(1.0 + 0.18 * jax.random.normal(splits[3], (DT,), jnp.float32), 0.1, 1.9)
    student_gain = jnp.clip(1.0 + 0.18 * jax.random.normal(splits[4], (DS,), jnp.float32), 0.1, 1.9)
    return dict(teacher_rows=teacher_rows, student_rows=student_rows, projector=projector, teacher_gain=teacher_gain, student_gain=student_gain)


epsilon = 1e-05

def reference(teacher_rows, student_rows, projector, teacher_gain, student_gain):
    teacher_f32 = teacher_rows.astype(jnp.float32)
    inv_teacher = lax.rsqrt(lax.optimization_barrier(jnp.mean(teacher_f32 * teacher_f32, axis=-1, keepdims=True)) + epsilon)
    target = (teacher_f32 * inv_teacher * teacher_gain).astype(jnp.bfloat16)
    student_f32 = student_rows.astype(jnp.float32)
    inv_student = lax.rsqrt(lax.optimization_barrier(jnp.mean(student_f32 * student_f32, axis=-1, keepdims=True)) + epsilon)
    unit_rows = student_f32 * inv_student
    features = (unit_rows * student_gain).astype(jnp.bfloat16)
    prediction = jnp.dot(features, projector, preferred_element_type=jnp.float32)
    residual_err = prediction - target.astype(jnp.float32)
    error_bf16 = residual_err.astype(jnp.bfloat16)
    projector_grad = jnp.dot(features.T, error_bf16, preferred_element_type=jnp.float32) / math.sqrt(TOKENS)
    feature_grad = jnp.dot(error_bf16, projector.T, preferred_element_type=jnp.float32)
    upstream = feature_grad * student_gain
    inner_mean = lax.optimization_barrier(jnp.mean(upstream * unit_rows, axis=-1, keepdims=True))
    input_grad = inv_student * (upstream - unit_rows * inner_mean)
    return (projector_grad, input_grad)
```

```python
import math

import jax
import jax.numpy as jnp
from jax import lax
from jax.experimental import pallas as pl
from jax.experimental.pallas import tpu as pltpu
from jax.sharding import PartitionSpec as P

epsilon = 1e-05

MESH = pl.DeviceIdType.MESH
DT = 16384
DS = 8192
TOKENS = 1024
SECT = 2
NX = 4
NY = 4
NZH = 2
DP = NZH * NY * NX
QUADS = 2
INQ = 4
TENSOR = QUADS * INQ
ST = SECT * TENSOR
TOK = TOKENS // DP
WT = DT // ST
WS = DS // ST
WC = DT // DP
HC = WC // SECT
CHUNK = TENSOR * TOK
LANES = 128
SEMS = 120
F32 = jnp.float32
BF16 = jnp.bfloat16

N1, F1, F2, N2 = range(4)
NEAR = (N1, N2)


def kernel(
    teacher_hbm, student_hbm, proj_hbm, tgain_hbm, sgain_hbm,
    pgrad, igrad,
    teacher, student, proj, tgain, sgain,
    stat, stat2, total_send, total_far, raw_far, feats, tsend, trecv, part, yrecv, ssend, r1, acc, a_send, r2,
    errs, gnear, gfar, g1, hnear, hsend, hfar, g2near, g2last, g2far, zsend, zrecv,
    load_sems, send_sems, recv_sems,
):
    c = lax.axis_index("sect")
    d = lax.axis_index("dp")
    t = lax.axis_index("tensor")
    h, y, x = d // (NY * NX), (d // NX) % NY, d % NX
    qd, zi = t // INQ, t % INQ
    pa, pb = 1 - zi // 2, zi % 2
    st = c * TENSOR + t
    far = 1 - h
    yp, yb, xp, xb = y // 2, y % 2, x // 2, x % 2

    used = [0]
    sent = []

    def tickets(count):
        used[0] += count
        return range(used[0] - count, used[0])

    def dev(sect=None, dp=None, tensor=None):
        return {
            "sect": c if sect is None else sect,
            "dp": d if dp is None else dp,
            "tensor": t if tensor is None else tensor,
        }

    def send(i, src, dst, to, recv=None):
        op = pltpu.make_async_remote_copy(
            src_ref=src, dst_ref=dst, send_sem=send_sems.at[i],
            recv_sem=recv_sems.at[i if recv is None else recv],
            device_id=to, device_id_type=MESH,
        )
        op.start()
        sent.append(op)

    def arrived(i, dst, to):
        pltpu.make_async_remote_copy(
            src_ref=dst, dst_ref=dst, send_sem=send_sems.at[i], recv_sem=recv_sems.at[i],
            device_id=to, device_id_type=MESH,
        ).wait_recv()

    def at(zh, yy, xx):
        return dev(dp=zh * (NY * NX) + yy * NX + xx)

    def x_plus(k):
        return (x + k) % NX

    def y_plus(k):
        return (y + k) % NY

    y_mate, x_mate = y + 1 - 2 * yb, x + 1 - 2 * xb
    z_mate = at(far, y, x)
    sibling = dev(sect=1 - c)
    across = dev(tensor=(1 - qd) * INQ + zi)

    def in_quad(k):
        return dev(tensor=qd * INQ + (zi + k) % INQ)

    def place(k):
        other = (zi + k) % INQ
        return 1 - other // 2, other % 2

    def st_dev(k):
        other = (st + k) % ST
        return other, dev(sect=other // TENSOR, tensor=other % TENSOR)

    loads = [
        pltpu.make_async_copy(src, dst, load_sems.at[i])
        for i, (src, dst) in enumerate(
            ((student_hbm, student), (teacher_hbm, teacher), (sgain_hbm, sgain), (tgain_hbm, tgain), (proj_hbm, proj))
        )
    ]
    for op in loads:
        op.start()

    barrier = pltpu.get_barrier_semaphore()

    def hello(to):
        pl.semaphore_signal(barrier, inc=1, device_id=to, device_id_type=MESH)

    for k in range(1, ST):
        hello(st_dev(k)[1])
    for k in range(1, NY * NX):
        hello(at(h, y_plus(k // NX), x_plus(k % NX)))
    hello(z_mate)
    source = dict(sect=(d // 2) // TENSOR, tensor=(d // 2) % TENSOR)
    for zh, yy, xx in (
        (h, 2 * yp + pa, 2 * qd + pb),
        (far, 2 * pa + qd, 2 * xp + pb),
        (far, 2 * pa + qd, 2 * (1 - xp) + pb),
        (h, 2 * (1 - yp) + pa, 2 * qd + pb),
    ):
        hello(dev(dp=zh * (NY * NX) + yy * NX + xx, **source))

    rows = lax.broadcasted_iota(jnp.int32, (TOK, LANES), 0)
    lanes = lax.broadcasted_iota(jnp.int32, (TOK, LANES), 1)
    zero = jnp.zeros((TOK, LANES), F32)

    def column(row, first):
        return jnp.sum(jnp.where(lanes == rows + first, row, zero), axis=1, keepdims=True)

    loads[0].wait()
    sf = student[...].astype(F32)
    ssum = jnp.sum(sf * sf, axis=1, keepdims=True)
    loads[1].wait()
    tf = teacher[...].astype(F32)
    tsum = jnp.sum(tf * tf, axis=1, keepdims=True)
    spread = jnp.where(lanes == rows, tsum, zero) + jnp.where(lanes == rows + TOK, ssum, zero)
    stat[st] = jnp.sum(spread, axis=0, keepdims=True)

    pl.semaphore_wait(barrier, (ST - 1) + (NY * NX - 1) + 1 + 4)

    def exchange(ref):
        own = tickets(ST - 1)
        for k in range(1, ST):
            send(own[k - 1], ref.at[st], ref.at[st], st_dev(k)[1])

        def finish():
            for k in range(1, ST):
                other, where = st_dev(ST - k)
                arrived(own[k - 1], ref.at[other], where)
            return jnp.sum(ref[...], axis=0)

        return finish

    finish_stat = exchange(stat)
    raw_t, total_t = tickets(2)
    send(raw_t, student, raw_far, z_mate)

    loads[2].wait()
    sg = sgain[st]
    sg_row = jnp.concatenate([sg[k : k + 1, :] for k in range(WS // LANES)], axis=1)
    loads[3].wait()
    tg = tgain[st]

    total = finish_stat()
    inv_s = lax.rsqrt(column(total, TOK) / DS + epsilon)
    unit = sf * inv_s
    feats[h, y, x] = (unit * sg_row).astype(BF16)
    nx_t, nm_t = tickets(NX - 1), tickets(NX)
    for k in range(1, NX):
        send(nx_t[k - 1], feats.at[h, y, x], feats.at[h, y, x], at(h, y, x_plus(k)))
    for k in range(NX):
        send(nm_t[k], feats.at[h, y, x], feats.at[h, y, x], at(h, y_mate, x_plus(k)))
    total_send[...] = total
    send(total_t, total_send, total_far, z_mate)

    inv_t = lax.rsqrt(column(total, 0) / DT + epsilon)
    for k in range(WT // LANES):
        col = k * LANES
        value = tf[:, col : col + LANES] * inv_t * tg[k : k + 1, :]
        tsend[col // WC, (col % WC) // HC, :, col % HC : col % HC + LANES] = value.astype(BF16)

    ny_t = tickets(2)
    tt = tickets(4)
    ts = tickets(4)
    near_there = h == c
    to_a = jnp.where(near_there, yb, yp)
    to_q = jnp.where(near_there, xp, yb)
    for j in range(2):
        xp_there = ((2 * t + j) % NX) // 2
        yp_there = t // INQ
        slot = jnp.where(
            near_there,
            jnp.where(yp == yp_there, N1, N2),
            jnp.where(xp == xp_there, F1, F2),
        )
        for u in range(SECT):
            send(
                ts[2 * j + u], tsend.at[j, u], trecv.at[slot],
                dev(sect=u, dp=2 * st + j, tensor=to_q * INQ + (1 - to_a) * 2 + xb),
                tt[0] + slot,
            )

    arrived(raw_t, raw_far, z_mate)
    arrived(total_t, total_far, z_mate)
    inv_far = lax.rsqrt(column(total_far[...], TOK) / DS + epsilon)
    feats[far, y, x] = (raw_far[...].astype(F32) * inv_far * sg_row).astype(BF16)
    fy_t = tickets(NY - 1)
    for k in range(1, NY):
        send(fy_t[k - 1], feats.at[far, y, x], feats.at[far, y, x], at(h, y_plus(k), x))

    fx_t = tickets(3)

    def rows_of(ci):
        if ci in NEAR:
            return feats[h, pl.ds(2 * (yp if ci == N1 else 1 - yp), 2)].reshape(CHUNK, WS)
        return feats[far, :, pl.ds(2 * (xp if ci == F1 else 1 - xp), 2)].reshape(CHUNK, WS)

    def features_ready(ci):
        if ci == N1:
            for k in range(1, NX):
                xx = x_plus(NX - k)
                arrived(nx_t[k - 1], feats.at[h, y, xx], at(h, y, xx))
            for r in range(2):
                send(ny_t[r], feats.at[h, y], feats.at[h, y], at(h, 2 * (1 - yp) + r, x), ny_t[0] + yb)
            for k in range(NX):
                xx = x_plus(NX - k)
                arrived(nm_t[k], feats.at[h, y_mate, xx], at(h, y_mate, xx))
        elif ci == N2:
            for r in range(2):
                arrived(ny_t[r], feats.at[h, 2 * (1 - yp) + r], at(h, 2 * (1 - yp) + r, x))
        elif ci == F1:
            arrived(fx_t[0], feats.at[far, :, x_mate], at(h, y, x_mate))
            for r in range(2):
                send(
                    fx_t[1 + r], feats.at[far, :, x], feats.at[far, :, x], at(h, y, 2 * (1 - xp) + r), fx_t[1] + xb
                )
        else:
            for r in range(2):
                arrived(fx_t[1 + r], feats.at[far, :, 2 * (1 - xp) + r], at(h, y, 2 * (1 - xp) + r))

    def far_columns():
        for k in range(1, NY):
            yy = y_plus(NY - k)
            arrived(fy_t[k - 1], feats.at[far, yy, x], at(h, yy, x))
        send(fx_t[0], feats.at[far, :, x], feats.at[far, :, x], at(h, y, x_mate))

    pair_t, r1_t, r2_t = tickets(4), [tickets(INQ - 1) for _ in range(4)], tickets(4)
    e2_t, es_t = [tickets(INQ - 1) for _ in range(4)], tickets(4)
    g1_t = [tickets(3) for _ in range(3)]
    n2_t, f2_t, last_t = tickets(1), tickets(3), tickets(2 * NX)
    (z_t,) = tickets(1)

    def predict(ci):
        features_ready(ci)
        value = rows_of(ci)
        for u in range(SECT):
            half = jnp.dot(value, proj[:, u * HC : (u + 1) * HC], preferred_element_type=F32)
            part[ci, u] = half.reshape(2, 2, 2, TOK, HC)
        send(pair_t[ci], part.at[ci, 1 - c], yrecv.at[ci], sibling)

    def sum_pair(ci):
        arrived(pair_t[ci], yrecv.at[ci], sibling)
        value = part[ci, c] + yrecv[ci]
        part[ci, c] = value
        ssend[ci] = value.astype(BF16)
        for k in range(1, INQ):
            a, b = place(k)
            send(r1_t[ci][k - 1], ssend.at[ci, a, :, b], r1.at[ci, k - 1], in_quad(k))

    def sum_quad(ci):
        for k in range(1, INQ):
            arrived(r1_t[ci][k - 1], r1.at[ci, k - 1], in_quad(INQ - k))
        value = part[ci, c, pa, :, pb]
        for k in range(INQ - 1):
            value = value + r1[ci, k].astype(F32)
        acc[ci] = value
        arrived(tt[ci], trecv.at[ci], sibling)
        acc[ci, qd] = acc[ci, qd] - trecv[ci].astype(F32)
        a_send[ci] = acc[ci].astype(BF16)
        send(r2_t[ci], a_send.at[ci], r2.at[ci], across)

    def residual(ci):
        arrived(r2_t[ci], r2.at[ci], across)
        errs[ci, c, pa, :, pb] = (acc[ci] + r2[ci].astype(F32)).astype(BF16)
        for k in range(1, INQ):
            send(e2_t[ci][k - 1], errs.at[ci, c, pa, :, pb], errs.at[ci, c, pa, :, pb], in_quad(k))

    def errors_pair(ci):
        for k in range(1, INQ):
            a, b = place(INQ - k)
            arrived(e2_t[ci][k - 1], errs.at[ci, c, a, :, b], in_quad(INQ - k))
        send(es_t[ci], errs.at[ci, c], errs.at[ci, c], sibling)

    def back(ci):
        arrived(es_t[ci], errs.at[ci, 1 - c], sibling)
        value = None
        for u in range(SECT):
            term = lax.dot_general(
                errs[ci, u].reshape(CHUNK, HC), proj[:, u * HC : (u + 1) * HC], (((1,), (1,)), ((), ())),
                preferred_element_type=F32,
            )
            value = term if value is None else value + term
        value = value.astype(BF16)
        if ci in NEAR:
            gnear[NEAR.index(ci)] = value.reshape(2, NX, TOK, WS)
            if ci == N2:
                for r in range(2):
                    for k in range(NX):
                        xx = x_plus(k)
                        send(
                            last_t[NX * r + k], gnear.at[1, r, xx], g2last.at[NX * yb + k],
                            at(h, 2 * (1 - yp) + r, xx), last_t[0] + NX * yb + k,
                        )
                return
            for k in range(1, NX):
                xx = x_plus(k)
                send(g1_t[ci][k - 1], gnear.at[NEAR.index(ci), :, xx], g1.at[ci, k - 1], at(h, y, xx))
        else:
            gfar[ci - F1] = value.reshape(NY, 2, TOK, WS)
            for k in range(1, NY):
                yy = y_plus(k)
                send(g1_t[ci][k - 1], gfar.at[ci - F1, yy], g1.at[ci, k - 1], at(h, yy, x))

    def grad(ci):
        for u in range(SECT):
            term = lax.dot_general(
                rows_of(ci), errs[ci, u].reshape(CHUNK, HC), (((0,), (0,)), ((), ())), preferred_element_type=F32
            ) * (1.0 / math.sqrt(TOKENS))
            cols = slice(u * HC, (u + 1) * HC)
            pgrad[:, cols] = term if ci == N1 else pgrad[:, cols] + term

    def second(ci):
        for k in range(1, 4):
            where = at(h, y, x_plus(NX - k)) if ci in NEAR else at(h, y_plus(NY - k), x)
            arrived(g1_t[ci][k - 1], g1.at[ci, k - 1], where)
        value = gnear[NEAR.index(ci), :, x] if ci in NEAR else gfar[ci - F1, y]
        value = value.astype(F32)
        for k in range(3):
            value = value + g1[ci, k].astype(F32)
        if ci == N1:
            hnear[...] = value
            hsend[...] = value.astype(BF16)
            send(n2_t[0], hsend.at[1 - yb], g2near, at(h, y_mate, x))
        else:
            f = ci - F1
            hfar[f] = value
            if ci == F1:
                send(f2_t[0], hfar.at[f, 1 - xb], g2far.at[0], at(h, y, x_mate))
            else:
                for r in range(2):
                    send(f2_t[1 + r], hfar.at[f, r], g2far.at[1 + xb], at(h, y, 2 * (1 - xp) + r), f2_t[1] + xb)

    def send_far():
        arrived(f2_t[0], g2far.at[0], at(h, y, x_mate))
        for r in range(2):
            arrived(f2_t[1 + r], g2far.at[1 + r], at(h, y, 2 * (1 - xp) + r))
        zsend[...] = (hfar[0, xb] + g2far[0] + g2far[1] + g2far[2]).astype(BF16)
        send(z_t, zsend, zrecv, z_mate)

    loads[4].wait()
    predict(N1)
    far_columns()
    sum_pair(N1)
    sum_quad(N1)
    predict(F1)
    residual(N1)
    sum_pair(F1)
    predict(F2)
    sum_quad(F1)
    sum_pair(F2)
    errors_pair(N1)
    predict(N2)
    residual(F1)
    back(N1)
    sum_quad(F2)
    sum_pair(N2)
    grad(N1)
    errors_pair(F1)
    residual(F2)
    sum_quad(N2)
    back(F1)
    second(N1)
    grad(F1)
    errors_pair(F2)
    residual(N2)
    back(F2)
    second(F1)
    grad(F2)
    errors_pair(N2)
    second(F2)
    back(N2)
    send_far()
    grad(N2)

    for op in sent:
        op.wait_send()
    sent.clear()

    arrived(n2_t[0], g2near, at(h, y_mate, x))
    arrived(z_t, zrecv, z_mate)
    feature_grad = hnear[yb] + g2near[...].astype(F32) + zrecv[...].astype(F32)
    for r in range(2):
        for k in range(NX):
            slot = NX * r + k
            arrived(last_t[slot], g2last.at[slot], at(h, 2 * (1 - yp) + r, x_plus(NX - k)))
            feature_grad = feature_grad + g2last[slot].astype(F32)
    upstream = feature_grad * sg_row

    inner = jnp.sum(upstream * unit, axis=1, keepdims=True)
    stat2[st] = jnp.sum(jnp.where(lanes == rows, inner, zero), axis=0, keepdims=True)
    inner_mean = column(exchange(stat2)(), 0) / DS
    igrad[...] = inv_s * (upstream - unit * inner_mean)

    for op in sent:
        op.wait_send()
    assert used[0] <= SEMS, used


def body(teacher_rows, student_rows, projector, teacher_gain, student_gain):
    vmem = pl.BlockSpec(memory_space=pltpu.VMEM)
    piece = (2, 2, 2, TOK, HC)
    return pl.pallas_call(
        kernel,
        out_shape=(
            jax.ShapeDtypeStruct((WS, WC), F32),
            jax.ShapeDtypeStruct((TOK, WS), F32),
        ),
        in_specs=[pl.BlockSpec(memory_space=pltpu.HBM)] * 5,
        out_specs=(vmem, vmem),
        scratch_shapes=[
            pltpu.VMEM((TOK, WT), BF16),
            pltpu.VMEM((TOK, WS), BF16),
            pltpu.VMEM((WS, WC), BF16),
            pltpu.VMEM((ST, WT // LANES, LANES), F32),
            pltpu.VMEM((ST, WS // LANES, LANES), F32),
            pltpu.VMEM((ST, 1, LANES), F32),
            pltpu.VMEM((ST, 1, LANES), F32),
            pltpu.VMEM((1, LANES), F32),
            pltpu.VMEM((1, LANES), F32),
            pltpu.VMEM((TOK, WS), BF16),
            pltpu.VMEM((NZH, NY, NX, TOK, WS), BF16),
            pltpu.VMEM((2, SECT, TOK, HC), BF16),
            pltpu.VMEM((4, TOK, HC), BF16),
            pltpu.VMEM((4, SECT) + piece, F32),
            pltpu.VMEM((4,) + piece, F32),
            pltpu.VMEM((4,) + piece, BF16),
            pltpu.VMEM((4, INQ - 1, QUADS, TOK, HC), BF16),
            pltpu.VMEM((4, QUADS, TOK, HC), F32),
            pltpu.VMEM((4, QUADS, TOK, HC), BF16),
            pltpu.VMEM((4, QUADS, TOK, HC), BF16),
            pltpu.VMEM((4, SECT) + piece, BF16),
            pltpu.VMEM((2, 2, NX, TOK, WS), BF16),
            pltpu.VMEM((2, NY, 2, TOK, WS), BF16),
            pltpu.VMEM((3, 3, 2, TOK, WS), BF16),
            pltpu.VMEM((2, TOK, WS), F32),
            pltpu.VMEM((2, TOK, WS), BF16),
            pltpu.VMEM((2, 2, TOK, WS), F32),
            pltpu.VMEM((TOK, WS), BF16),
            pltpu.VMEM((2 * NX, TOK, WS), BF16),
            pltpu.VMEM((3, TOK, WS), F32),
            pltpu.VMEM((TOK, WS), BF16),
            pltpu.VMEM((TOK, WS), BF16),
            pltpu.SemaphoreType.DMA((5,)),
            pltpu.SemaphoreType.DMA((SEMS,)),
            pltpu.SemaphoreType.DMA((SEMS,)),
        ],
        compiler_params=pltpu.CompilerParams(
            collective_id=0, has_side_effects=True, vmem_limit_bytes=32 * 1024 * 1024
        ),
    )(
        teacher_rows,
        student_rows,
        projector,
        teacher_gain.reshape(ST, WT // LANES, LANES),
        student_gain.reshape(ST, WS // LANES, LANES),
    )


def solution(mesh):
    return jax.shard_map(
        body,
        mesh=mesh,
        in_specs=(
            P("dp", ("sect", "tensor")),
            P("dp", ("sect", "tensor")),
            P(("sect", "tensor"), "dp"),
            P(),
            P(),
        ),
        out_specs=(P(("sect", "tensor"), "dp"), P("dp", ("sect", "tensor"))),
        check_vma=False,
    )
```

```python
import math

import jax
import jax.numpy as jnp
from jax import lax
from jax.experimental import pallas as pl
from jax.experimental.pallas import tpu as pltpu
from jax.sharding import PartitionSpec as P

epsilon = 1e-05

MESH = pl.DeviceIdType.MESH
DT = 16384
DS = 8192
TOKENS = 1024
SECT = 2
NX = 4
NY = 4
NZH = 2
DP = NZH * NY * NX
QUADS = 2
INQ = 4
TENSOR = QUADS * INQ
ST = SECT * TENSOR
TOK = TOKENS // DP
WT = DT // ST
WS = DS // ST
WC = DT // DP
HC = WC // SECT
CHUNK = TENSOR * TOK
LANES = 128
SEMS = 120
F32 = jnp.float32
BF16 = jnp.bfloat16

N1, F1, F2, N2 = range(4)
NEAR = (N1, N2)


def kernel(
    teacher_hbm, student_hbm, proj_hbm, tgain_hbm, sgain_hbm,
    pgrad_hbm, igrad_hbm,
    pgrad, igrad, pt, ft, teacher, student, proj, tgain, sgain,
    stat, stat2, total_send, total_far, raw_far, feats, tsend, trecv, part, yrecv, ssend, r1, acc, a_send, r2,
    errs, gnear, gfar, g1, hnear, hsend, hfar, g2near, g2last, g2far, zsend, zrecv,
    load_sems, send_sems, recv_sems,
):
    c = lax.axis_index("sect")
    d = lax.axis_index("dp")
    t = lax.axis_index("tensor")
    h, y, x = d // (NY * NX), (d // NX) % NY, d % NX
    qd, zi = t // INQ, t % INQ
    pa, pb = 1 - zi // 2, zi % 2
    st = c * TENSOR + t
    far = 1 - h
    yp, yb, xp, xb = y // 2, y % 2, x // 2, x % 2

    used = [0]
    sent = []

    def tickets(count):
        used[0] += count
        return range(used[0] - count, used[0])

    def dev(sect=None, dp=None, tensor=None):
        return {
            "sect": c if sect is None else sect,
            "dp": d if dp is None else dp,
            "tensor": t if tensor is None else tensor,
        }

    def send(i, src, dst, to, recv=None):
        op = pltpu.make_async_remote_copy(
            src_ref=src, dst_ref=dst, send_sem=send_sems.at[i],
            recv_sem=recv_sems.at[i if recv is None else recv],
            device_id=to, device_id_type=MESH,
        )
        op.start()
        sent.append(op)

    def arrived(i, dst, to):
        pltpu.make_async_remote_copy(
            src_ref=dst, dst_ref=dst, send_sem=send_sems.at[i], recv_sem=recv_sems.at[i],
            device_id=to, device_id_type=MESH,
        ).wait_recv()

    def at(zh, yy, xx):
        return dev(dp=zh * (NY * NX) + yy * NX + xx)

    def x_plus(k):
        return (x + k) % NX

    def y_plus(k):
        return (y + k) % NY

    y_mate, x_mate = y + 1 - 2 * yb, x + 1 - 2 * xb
    z_mate = at(far, y, x)
    sibling = dev(sect=1 - c)
    across = dev(tensor=(1 - qd) * INQ + zi)

    def in_quad(k):
        return dev(tensor=qd * INQ + (zi + k) % INQ)

    def place(k):
        other = (zi + k) % INQ
        return 1 - other // 2, other % 2

    def st_dev(k):
        other = (st + k) % ST
        return other, dev(sect=other // TENSOR, tensor=other % TENSOR)

    loads = [
        pltpu.make_async_copy(src, dst, load_sems.at[i])
        for i, (src, dst) in enumerate(
            ((student_hbm, student), (teacher_hbm, teacher), (sgain_hbm, sgain), (tgain_hbm, tgain), (proj_hbm, proj))
        )
    ]
    for op in loads:
        op.start()

    barrier = pltpu.get_barrier_semaphore()

    def hello(to):
        pl.semaphore_signal(barrier, inc=1, device_id=to, device_id_type=MESH)

    for k in range(1, ST):
        hello(st_dev(k)[1])
    for k in range(1, NY * NX):
        hello(at(h, y_plus(k // NX), x_plus(k % NX)))
    hello(z_mate)
    source = dict(sect=(d // 2) // TENSOR, tensor=(d // 2) % TENSOR)
    for zh, yy, xx in (
        (h, 2 * yp + pa, 2 * qd + pb),
        (far, 2 * pa + qd, 2 * xp + pb),
        (far, 2 * pa + qd, 2 * (1 - xp) + pb),
        (h, 2 * (1 - yp) + pa, 2 * qd + pb),
    ):
        hello(dev(dp=zh * (NY * NX) + yy * NX + xx, **source))

    rows = lax.broadcasted_iota(jnp.int32, (TOK, LANES), 0)
    lanes = lax.broadcasted_iota(jnp.int32, (TOK, LANES), 1)
    zero = jnp.zeros((TOK, LANES), F32)

    def column(row, first):
        return jnp.sum(jnp.where(lanes == rows + first, row, zero), axis=1, keepdims=True)

    loads[0].wait()
    sf = student[...].astype(F32)
    ssum = jnp.sum(sf * sf, axis=1, keepdims=True)
    loads[1].wait()
    tf = teacher[...].astype(F32)
    tsum = jnp.sum(tf * tf, axis=1, keepdims=True)
    spread = jnp.where(lanes == rows, tsum, zero) + jnp.where(lanes == rows + TOK, ssum, zero)
    stat[st] = jnp.sum(spread, axis=0, keepdims=True)

    pl.semaphore_wait(barrier, (ST - 1) + (NY * NX - 1) + 1 + 4)

    def exchange(ref):
        own = tickets(ST - 1)
        for k in range(1, ST):
            send(own[k - 1], ref.at[st], ref.at[st], st_dev(k)[1])

        def finish():
            for k in range(1, ST):
                other, where = st_dev(ST - k)
                arrived(own[k - 1], ref.at[other], where)
            return jnp.sum(ref[...], axis=0)

        return finish

    finish_stat = exchange(stat)
    raw_t, total_t = tickets(2)
    send(raw_t, student, raw_far, z_mate)

    loads[2].wait()
    sg = sgain[st]
    sg_row = jnp.concatenate([sg[k : k + 1, :] for k in range(WS // LANES)], axis=1)
    loads[3].wait()
    tg = tgain[st]

    loads[4].wait()
    pt[...] = proj[...].T

    total = finish_stat()
    inv_s = lax.rsqrt(column(total, TOK) / DS + epsilon)
    unit = sf * inv_s
    feats[h, y, x] = (unit * sg_row).astype(BF16)
    nx_t, nm_t = tickets(NX - 1), tickets(NX)
    for k in range(1, NX):
        send(nx_t[k - 1], feats.at[h, y, x], feats.at[h, y, x], at(h, y, x_plus(k)))
    for k in range(NX):
        send(nm_t[k], feats.at[h, y, x], feats.at[h, y, x], at(h, y_mate, x_plus(k)))
    total_send[...] = total
    send(total_t, total_send, total_far, z_mate)

    inv_t = lax.rsqrt(column(total, 0) / DT + epsilon)
    for k in range(WT // LANES):
        col = k * LANES
        value = tf[:, col : col + LANES] * inv_t * tg[k : k + 1, :]
        tsend[col // WC, (col % WC) // HC, :, col % HC : col % HC + LANES] = value.astype(BF16)

    ny_t = tickets(2)
    tt = tickets(4)
    ts = tickets(4)
    rows_out = []
    near_there = h == c
    to_a = jnp.where(near_there, yb, yp)
    to_q = jnp.where(near_there, xp, yb)
    for j in range(2):
        xp_there = ((2 * t + j) % NX) // 2
        yp_there = t // INQ
        slot = jnp.where(
            near_there,
            jnp.where(yp == yp_there, N1, N2),
            jnp.where(xp == xp_there, F1, F2),
        )
        for u in range(SECT):
            rows_out.append(
                pltpu.make_async_remote_copy(
                    src_ref=tsend.at[j, u], dst_ref=trecv.at[slot],
                    send_sem=send_sems.at[ts[2 * j + u]], recv_sem=recv_sems.at[tt[0] + slot],
                    device_id=dev(sect=u, dp=2 * st + j, tensor=to_q * INQ + (1 - to_a) * 2 + xb),
                    device_id_type=MESH,
                )
            )

    first_chunk = jnp.logical_and(near_there, yp == t // INQ)

    def send_teacher(now):
        @pl.when(now)
        def _():
            for op in rows_out:
                op.start()

    send_teacher(first_chunk)

    arrived(raw_t, raw_far, z_mate)
    arrived(total_t, total_far, z_mate)
    inv_far = lax.rsqrt(column(total_far[...], TOK) / DS + epsilon)
    feats[far, y, x] = (raw_far[...].astype(F32) * inv_far * sg_row).astype(BF16)
    fy_t = tickets(NY - 1)
    for k in range(1, NY):
        send(fy_t[k - 1], feats.at[far, y, x], feats.at[far, y, x], at(h, y_plus(k), x))

    fx_t = tickets(3)

    def rows_of(ci):
        if ci in NEAR:
            return feats[h, pl.ds(2 * (yp if ci == N1 else 1 - yp), 2)].reshape(CHUNK, WS)
        return feats[far, :, pl.ds(2 * (xp if ci == F1 else 1 - xp), 2)].reshape(CHUNK, WS)

    def features_ready(ci):
        if ci == N1:
            for k in range(1, NX):
                xx = x_plus(NX - k)
                arrived(nx_t[k - 1], feats.at[h, y, xx], at(h, y, xx))
            for k in range(NX):
                xx = x_plus(NX - k)
                arrived(nm_t[k], feats.at[h, y_mate, xx], at(h, y_mate, xx))
        elif ci == N2:
            for r in range(2):
                arrived(ny_t[r], feats.at[h, 2 * (1 - yp) + r], at(h, 2 * (1 - yp) + r, x))
        elif ci == F1:
            arrived(fx_t[0], feats.at[far, :, x_mate], at(h, y, x_mate))
            for r in range(2):
                send(
                    fx_t[1 + r], feats.at[far, :, x], feats.at[far, :, x], at(h, y, 2 * (1 - xp) + r), fx_t[1] + xb
                )
        else:
            for r in range(2):
                arrived(fx_t[1 + r], feats.at[far, :, 2 * (1 - xp) + r], at(h, y, 2 * (1 - xp) + r))

    def far_columns():
        for k in range(1, NY):
            yy = y_plus(NY - k)
            arrived(fy_t[k - 1], feats.at[far, yy, x], at(h, yy, x))
        send(fx_t[0], feats.at[far, :, x], feats.at[far, :, x], at(h, y, x_mate))

    def near_rows():
        for r in range(2):
            send(ny_t[r], feats.at[h, y], feats.at[h, y], at(h, 2 * (1 - yp) + r, x), ny_t[0] + yb)

    pair_t, r1_t, r2_t = tickets(4), [tickets(INQ - 1) for _ in range(4)], tickets(4)
    e2_t, es_t = [tickets(INQ - 1) for _ in range(4)], tickets(4)
    g1_t = [tickets(3) for _ in range(3)]
    n2_t, f2_t, last_t = tickets(1), tickets(3), tickets(2 * NX)
    (z_t,) = tickets(1)

    def predict(ci):
        features_ready(ci)
        value = rows_of(ci)
        for u in range(SECT):
            half = jnp.dot(value, proj[:, u * HC : (u + 1) * HC], preferred_element_type=F32)
            part[ci, u] = half.reshape(2, 2, 2, TOK, HC)
        send(pair_t[ci], part.at[ci, 1 - c], yrecv.at[ci], sibling)

    def sum_pair(ci):
        arrived(pair_t[ci], yrecv.at[ci], sibling)
        value = part[ci, c] + yrecv[ci]
        part[ci, c] = value
        ssend[ci] = value.astype(BF16)
        for k in range(1, INQ):
            a, b = place(k)
            send(r1_t[ci][k - 1], ssend.at[ci, a, :, b], r1.at[ci, k - 1], in_quad(k))

    def sum_quad(ci):
        for k in range(1, INQ):
            arrived(r1_t[ci][k - 1], r1.at[ci, k - 1], in_quad(INQ - k))
        value = part[ci, c, pa, :, pb]
        for k in range(INQ - 1):
            value = value + r1[ci, k].astype(F32)
        acc[ci] = value
        arrived(tt[ci], trecv.at[ci], sibling)
        acc[ci, qd] = acc[ci, qd] - trecv[ci].astype(F32)
        a_send[ci] = acc[ci].astype(BF16)
        send(r2_t[ci], a_send.at[ci], r2.at[ci], across)

    def residual(ci):
        arrived(r2_t[ci], r2.at[ci], across)
        errs[ci, c, pa, :, pb] = (acc[ci] + r2[ci].astype(F32)).astype(BF16)
        for k in range(1, INQ):
            send(e2_t[ci][k - 1], errs.at[ci, c, pa, :, pb], errs.at[ci, c, pa, :, pb], in_quad(k))

    def errors_pair(ci):
        for k in range(1, INQ):
            a, b = place(INQ - k)
            arrived(e2_t[ci][k - 1], errs.at[ci, c, a, :, b], in_quad(INQ - k))
        send(es_t[ci], errs.at[ci, c], errs.at[ci, c], sibling)

    def back(ci):
        arrived(es_t[ci], errs.at[ci, 1 - c], sibling)
        value = None
        for u in range(SECT):
            term = jnp.dot(
                errs[ci, u].reshape(CHUNK, HC), pt[u * HC : (u + 1) * HC, :], preferred_element_type=F32
            )
            value = term if value is None else value + term
        value = value.astype(BF16)
        if ci in NEAR:
            gnear[NEAR.index(ci)] = value.reshape(2, NX, TOK, WS)
            if ci == N2:
                for r in range(2):
                    for k in range(NX):
                        xx = x_plus(k)
                        send(
                            last_t[NX * r + k], gnear.at[1, r, xx], g2last.at[NX * yb + k],
                            at(h, 2 * (1 - yp) + r, xx), last_t[0] + NX * yb + k,
                        )
                return
            for k in range(1, NX):
                xx = x_plus(k)
                send(g1_t[ci][k - 1], gnear.at[NEAR.index(ci), :, xx], g1.at[ci, k - 1], at(h, y, xx))
        else:
            gfar[ci - F1] = value.reshape(NY, 2, TOK, WS)
            for k in range(1, NY):
                yy = y_plus(k)
                send(g1_t[ci][k - 1], gfar.at[ci - F1, yy], g1.at[ci, k - 1], at(h, yy, x))

    def turn(ci):
        ft[ci] = rows_of(ci).T

    def grad(ci):
        for u in range(SECT):
            term = jnp.dot(ft[ci], errs[ci, u].reshape(CHUNK, HC), preferred_element_type=F32)
            cols = slice(u * HC, (u + 1) * HC)
            pgrad[:, cols] = term if ci == N1 else pgrad[:, cols] + term

    def second(ci):
        for k in range(1, 4):
            where = at(h, y, x_plus(NX - k)) if ci in NEAR else at(h, y_plus(NY - k), x)
            arrived(g1_t[ci][k - 1], g1.at[ci, k - 1], where)
        value = gnear[NEAR.index(ci), :, x] if ci in NEAR else gfar[ci - F1, y]
        value = value.astype(F32)
        for k in range(3):
            value = value + g1[ci, k].astype(F32)
        if ci == N1:
            hnear[...] = value
            hsend[...] = value.astype(BF16)
            send(n2_t[0], hsend.at[1 - yb], g2near, at(h, y_mate, x))
        else:
            f = ci - F1
            hfar[f] = value
            if ci == F1:
                send(f2_t[0], hfar.at[f, 1 - xb], g2far.at[0], at(h, y, x_mate))
            else:
                for r in range(2):
                    send(f2_t[1 + r], hfar.at[f, r], g2far.at[1 + xb], at(h, y, 2 * (1 - xp) + r), f2_t[1] + xb)

    def send_far():
        arrived(f2_t[0], g2far.at[0], at(h, y, x_mate))
        for r in range(2):
            arrived(f2_t[1 + r], g2far.at[1 + r], at(h, y, 2 * (1 - xp) + r))
        zsend[...] = (hfar[0, xb] + g2far[0] + g2far[1] + g2far[2]).astype(BF16)
        send(z_t, zsend, zrecv, z_mate)

    store_pgrad = pltpu.make_async_copy(pgrad, pgrad_hbm, load_sems.at[5])
    store_igrad = pltpu.make_async_copy(igrad, igrad_hbm, load_sems.at[6])

    predict(N1)
    far_columns()
    sum_pair(N1)
    send_teacher(jnp.logical_not(first_chunk))
    turn(N1)
    predict(F1)
    near_rows()
    sum_quad(N1)
    sum_pair(F1)
    turn(F1)
    residual(N1)
    predict(F2)
    sum_quad(F1)
    sum_pair(F2)
    turn(F2)
    errors_pair(N1)
    predict(N2)
    residual(F1)
    back(N1)
    sum_quad(F2)
    sum_pair(N2)
    turn(N2)
    grad(N1)
    errors_pair(F1)
    residual(F2)
    sum_quad(N2)
    back(F1)
    second(N1)
    grad(F1)
    errors_pair(F2)
    residual(N2)
    back(F2)
    second(F1)
    grad(F2)
    errors_pair(N2)
    second(F2)
    back(N2)
    send_far()
    grad(N2)
    store_pgrad.start()
    sent.extend(rows_out)

    for op in sent:
        op.wait_send()
    sent.clear()

    arrived(n2_t[0], g2near, at(h, y_mate, x))
    arrived(z_t, zrecv, z_mate)
    feature_grad = hnear[yb] + g2near[...].astype(F32) + zrecv[...].astype(F32)
    for r in range(2):
        for k in range(NX):
            slot = NX * r + k
            arrived(last_t[slot], g2last.at[slot], at(h, 2 * (1 - yp) + r, x_plus(NX - k)))
            feature_grad = feature_grad + g2last[slot].astype(F32)
    upstream = feature_grad * sg_row

    inner = jnp.sum(upstream * unit, axis=1, keepdims=True)
    stat2[st] = jnp.sum(jnp.where(lanes == rows, inner, zero), axis=0, keepdims=True)
    inner_mean = column(exchange(stat2)(), 0) / DS
    igrad[...] = inv_s * (upstream - unit * inner_mean)
    store_igrad.start()

    for op in sent:
        op.wait_send()
    store_pgrad.wait()
    store_igrad.wait()
    assert used[0] <= SEMS, used


def body(teacher_rows, student_rows, projector, teacher_gain, student_gain):
    anywhere = pl.BlockSpec(memory_space=pl.ANY)
    piece = (2, 2, 2, TOK, HC)
    summed, input_grad = pl.pallas_call(
        kernel,
        out_shape=(
            jax.ShapeDtypeStruct((WS, WC), F32),
            jax.ShapeDtypeStruct((TOK, WS), F32),
        ),
        in_specs=[anywhere] * 5,
        out_specs=(anywhere, anywhere),
        scratch_shapes=[
            pltpu.VMEM((WS, WC), F32),
            pltpu.VMEM((TOK, WS), F32),
            pltpu.VMEM((WC, WS), BF16),
            pltpu.VMEM((4, WS, CHUNK), BF16),
            pltpu.VMEM((TOK, WT), BF16),
            pltpu.VMEM((TOK, WS), BF16),
            pltpu.VMEM((WS, WC), BF16),
            pltpu.VMEM((ST, WT // LANES, LANES), F32),
            pltpu.VMEM((ST, WS // LANES, LANES), F32),
            pltpu.VMEM((ST, 1, LANES), F32),
            pltpu.VMEM((ST, 1, LANES), F32),
            pltpu.VMEM((1, LANES), F32),
            pltpu.VMEM((1, LANES), F32),
            pltpu.VMEM((TOK, WS), BF16),
            pltpu.VMEM((NZH, NY, NX, TOK, WS), BF16),
            pltpu.VMEM((2, SECT, TOK, HC), BF16),
            pltpu.VMEM((4, TOK, HC), BF16),
            pltpu.VMEM((4, SECT) + piece, F32),
            pltpu.VMEM((4,) + piece, F32),
            pltpu.VMEM((4,) + piece, BF16),
            pltpu.VMEM((4, INQ - 1, QUADS, TOK, HC), BF16),
            pltpu.VMEM((4, QUADS, TOK, HC), F32),
            pltpu.VMEM((4, QUADS, TOK, HC), BF16),
            pltpu.VMEM((4, QUADS, TOK, HC), BF16),
            pltpu.VMEM((4, SECT) + piece, BF16),
            pltpu.VMEM((2, 2, NX, TOK, WS), BF16),
            pltpu.VMEM((2, NY, 2, TOK, WS), BF16),
            pltpu.VMEM((3, 3, 2, TOK, WS), BF16),
            pltpu.VMEM((2, TOK, WS), F32),
            pltpu.VMEM((2, TOK, WS), BF16),
            pltpu.VMEM((2, 2, TOK, WS), F32),
            pltpu.VMEM((TOK, WS), BF16),
            pltpu.VMEM((2 * NX, TOK, WS), BF16),
            pltpu.VMEM((3, TOK, WS), F32),
            pltpu.VMEM((TOK, WS), BF16),
            pltpu.VMEM((TOK, WS), BF16),
            pltpu.SemaphoreType.DMA((7,)),
            pltpu.SemaphoreType.DMA((SEMS,)),
            pltpu.SemaphoreType.DMA((SEMS,)),
        ],
        compiler_params=pltpu.CompilerParams(
            collective_id=0, has_side_effects=True, vmem_limit_bytes=56 * 1024 * 1024
        ),
    )(
        teacher_rows,
        student_rows,
        projector,
        teacher_gain.reshape(ST, WT // LANES, LANES),
        student_gain.reshape(ST, WS // LANES, LANES),
    )
    return summed * (1.0 / math.sqrt(TOKENS)), input_grad


def solution(mesh):
    return jax.shard_map(
        body,
        mesh=mesh,
        in_specs=(
            P("dp", ("sect", "tensor")),
            P("dp", ("sect", "tensor")),
            P(("sect", "tensor"), "dp"),
            P(),
            P(),
        ),
        out_specs=(P(("sect", "tensor"), "dp"), P("dp", ("sect", "tensor"))),
        check_vma=False,
    )
```

```python
import math

import jax
import jax.numpy as jnp
from jax import lax
from jax.experimental import pallas as pl
from jax.experimental.pallas import tpu as pltpu
from jax.sharding import PartitionSpec as P

epsilon = 1e-05

MESH = pl.DeviceIdType.MESH
DT = 16384
DS = 8192
TOKENS = 1024
SECT = 2
NX = 4
NY = 4
NZH = 2
DP = NZH * NY * NX
QUADS = 2
INQ = 4
TENSOR = QUADS * INQ
ST = SECT * TENSOR
TOK = TOKENS // DP
WT = DT // ST
WS = DS // ST
WC = DT // DP
HC = WC // SECT
CHUNK = TENSOR * TOK
LANES = 128
SEMS = 144
F32 = jnp.float32
BF16 = jnp.bfloat16

N1, F1, F2, N2 = range(4)
NEAR = (N1, N2)


def kernel(
    teacher_hbm, student_hbm, proj_hbm, tgain_hbm, sgain_hbm,
    pgrad_hbm, igrad_hbm,
    pgrad, igrad, pt, ft, teacher, student, proj, tgain, sgain,
    stat, stat2, total_send, total_far, raw_far, feats, tsend, trecv, part, yrecv, ssend, r1, acc, a_send, r2,
    errs, gnear, gfar, gnear_in, gfar_in, zsend, zrecv,
    load_sems, send_sems, recv_sems,
):
    c = lax.axis_index("sect")
    d = lax.axis_index("dp")
    t = lax.axis_index("tensor")
    h, y, x = d // (NY * NX), (d // NX) % NY, d % NX
    qd, zi = t // INQ, t % INQ
    pa, pb = 1 - zi // 2, zi % 2
    st = c * TENSOR + t
    far = 1 - h
    yp, yb, xp, xb = y // 2, y % 2, x // 2, x % 2

    used = [0]
    sent = []

    def tickets(count):
        used[0] += count
        return range(used[0] - count, used[0])

    def dev(sect=None, dp=None, tensor=None):
        return {
            "sect": c if sect is None else sect,
            "dp": d if dp is None else dp,
            "tensor": t if tensor is None else tensor,
        }

    def send(i, src, dst, to, recv=None):
        op = pltpu.make_async_remote_copy(
            src_ref=src, dst_ref=dst, send_sem=send_sems.at[i],
            recv_sem=recv_sems.at[i if recv is None else recv],
            device_id=to, device_id_type=MESH,
        )
        op.start()
        sent.append(op)

    def arrived(i, dst, to):
        pltpu.make_async_remote_copy(
            src_ref=dst, dst_ref=dst, send_sem=send_sems.at[i], recv_sem=recv_sems.at[i],
            device_id=to, device_id_type=MESH,
        ).wait_recv()

    def at(zh, yy, xx):
        return dev(dp=zh * (NY * NX) + yy * NX + xx)

    def x_plus(k):
        return (x + k) % NX

    def y_plus(k):
        return (y + k) % NY

    y_mate, x_mate = y + 1 - 2 * yb, x + 1 - 2 * xb
    z_mate = at(far, y, x)
    sibling = dev(sect=1 - c)
    across = dev(tensor=(1 - qd) * INQ + zi)

    def peers(ci):
        first, out = ci in (N1, F1), []
        for r in range(2):
            for k in range(4):
                if first and r == 0 and k == 0:
                    continue
                if ci in NEAR:
                    line = (y, y_mate)[r] if first else 2 * (1 - yp) + r
                    to, of, mine = (line, x_plus(k)), (line, x_plus(NX - k)), yb
                else:
                    line = (x, x_mate)[r] if first else 2 * (1 - xp) + r
                    to, of, mine = (y_plus(k), line), (y_plus(NY - k), line), xb
                here = 4 * r + k - 1 if first else 7 + 4 * r + k
                there = here if first else 7 + 4 * mine + k
                out.append((to, of, there, here))
        return out

    def in_quad(k):
        return dev(tensor=qd * INQ + (zi + k) % INQ)

    def place(k):
        other = (zi + k) % INQ
        return 1 - other // 2, other % 2

    def st_dev(k):
        other = (st + k) % ST
        return other, dev(sect=other // TENSOR, tensor=other % TENSOR)

    loads = [
        pltpu.make_async_copy(src, dst, load_sems.at[i])
        for i, (src, dst) in enumerate(
            ((student_hbm, student), (teacher_hbm, teacher), (sgain_hbm, sgain), (tgain_hbm, tgain), (proj_hbm, proj))
        )
    ]
    for op in loads:
        op.start()

    barrier = pltpu.get_barrier_semaphore()

    def hello(to):
        pl.semaphore_signal(barrier, inc=1, device_id=to, device_id_type=MESH)

    for k in range(1, ST):
        hello(st_dev(k)[1])
    for k in range(1, NY * NX):
        hello(at(h, y_plus(k // NX), x_plus(k % NX)))
    hello(z_mate)
    source = dict(sect=(d // 2) // TENSOR, tensor=(d // 2) % TENSOR)
    for zh, yy, xx in (
        (h, 2 * yp + pa, 2 * qd + pb),
        (far, 2 * pa + qd, 2 * xp + pb),
        (far, 2 * pa + qd, 2 * (1 - xp) + pb),
        (h, 2 * (1 - yp) + pa, 2 * qd + pb),
    ):
        hello(dev(dp=zh * (NY * NX) + yy * NX + xx, **source))

    rows = lax.broadcasted_iota(jnp.int32, (TOK, LANES), 0)
    lanes = lax.broadcasted_iota(jnp.int32, (TOK, LANES), 1)
    zero = jnp.zeros((TOK, LANES), F32)

    def column(row, first):
        return jnp.sum(jnp.where(lanes == rows + first, row, zero), axis=1, keepdims=True)

    loads[0].wait()
    sf = student[...].astype(F32)
    ssum = jnp.sum(sf * sf, axis=1, keepdims=True)
    loads[1].wait()
    tf = teacher[...].astype(F32)
    tsum = jnp.sum(tf * tf, axis=1, keepdims=True)
    spread = jnp.where(lanes == rows, tsum, zero) + jnp.where(lanes == rows + TOK, ssum, zero)
    stat[st] = jnp.sum(spread, axis=0, keepdims=True)

    pl.semaphore_wait(barrier, (ST - 1) + (NY * NX - 1) + 1 + 4)

    def exchange(ref):
        own = tickets(ST - 1)
        for k in range(1, ST):
            send(own[k - 1], ref.at[st], ref.at[st], st_dev(k)[1])

        def finish():
            for k in range(1, ST):
                other, where = st_dev(ST - k)
                arrived(own[k - 1], ref.at[other], where)
            return jnp.sum(ref[...], axis=0)

        return finish

    finish_stat = exchange(stat)
    raw_t, total_t = tickets(2)
    send(raw_t, student, raw_far, z_mate)

    loads[2].wait()
    sg = sgain[st]
    sg_row = jnp.concatenate([sg[k : k + 1, :] for k in range(WS // LANES)], axis=1)
    loads[3].wait()
    tg = tgain[st]

    loads[4].wait()
    pt[...] = proj[...].T

    total = finish_stat()
    inv_s = lax.rsqrt(column(total, TOK) / DS + epsilon)
    unit = sf * inv_s
    feats[h, y, x] = (unit * sg_row).astype(BF16)
    near_t, far_t = tickets(15), tickets(15)

    def spread(ci):
        zh, base = (h, near_t[0]) if ci in NEAR else (far, far_t[0])
        for to, _, there, here in peers(ci):
            send(base + here, feats.at[zh, y, x], feats.at[zh, y, x], at(h, *to), base + there)

    spread(N1)
    total_send[...] = total
    send(total_t, total_send, total_far, z_mate)
    spread(N2)

    inv_t = lax.rsqrt(column(total, 0) / DT + epsilon)
    for k in range(WT // LANES):
        col = k * LANES
        value = tf[:, col : col + LANES] * inv_t * tg[k : k + 1, :]
        tsend[col // WC, (col % WC) // HC, :, col % HC : col % HC + LANES] = value.astype(BF16)

    tt = tickets(4)
    ts = tickets(4)
    rows_out = []
    near_there = h == c
    to_a = jnp.where(near_there, yb, yp)
    to_q = jnp.where(near_there, xp, yb)
    for j in range(2):
        xp_there = ((2 * t + j) % NX) // 2
        yp_there = t // INQ
        slot = jnp.where(
            near_there,
            jnp.where(yp == yp_there, N1, N2),
            jnp.where(xp == xp_there, F1, F2),
        )
        for u in range(SECT):
            rows_out.append(
                pltpu.make_async_remote_copy(
                    src_ref=tsend.at[j, u], dst_ref=trecv.at[slot],
                    send_sem=send_sems.at[ts[2 * j + u]], recv_sem=recv_sems.at[tt[0] + slot],
                    device_id=dev(sect=u, dp=2 * st + j, tensor=to_q * INQ + (1 - to_a) * 2 + xb),
                    device_id_type=MESH,
                )
            )

    first_chunk = jnp.logical_and(near_there, yp == t // INQ)

    def send_teacher(now):
        @pl.when(now)
        def _():
            for op in rows_out:
                op.start()

    send_teacher(first_chunk)

    def far_in():
        arrived(raw_t, raw_far, z_mate)
        arrived(total_t, total_far, z_mate)
        inv_far = lax.rsqrt(column(total_far[...], TOK) / DS + epsilon)
        feats[far, y, x] = (raw_far[...].astype(F32) * inv_far * sg_row).astype(BF16)
        spread(F1)
        spread(F2)

    def rows_of(ci):
        if ci in NEAR:
            return feats[h, pl.ds(2 * (yp if ci == N1 else 1 - yp), 2)].reshape(CHUNK, WS)
        return feats[far, :, pl.ds(2 * (xp if ci == F1 else 1 - xp), 2)].reshape(CHUNK, WS)

    def features_ready(ci):
        zh, base = (h, near_t[0]) if ci in NEAR else (far, far_t[0])
        for _, of, _, here in peers(ci):
            arrived(base + here, feats.at[zh, of[0], of[1]], at(h, *of))

    pair_t, r1_t, r2_t = tickets(4), [tickets(INQ - 1) for _ in range(4)], tickets(4)
    e2_t, es_t = [tickets(INQ - 1) for _ in range(4)], tickets(4)
    gnear_t, gfar_t = tickets(15), tickets(15)
    (z_t,) = tickets(1)

    def predict(ci):
        features_ready(ci)
        value = rows_of(ci)
        for u in range(SECT):
            half = jnp.dot(value, proj[:, u * HC : (u + 1) * HC], preferred_element_type=F32)
            part[ci, u] = half.reshape(2, 2, 2, TOK, HC)
        send(pair_t[ci], part.at[ci, 1 - c], yrecv.at[ci], sibling)

    def sum_pair(ci):
        arrived(pair_t[ci], yrecv.at[ci], sibling)
        value = part[ci, c] + yrecv[ci]
        part[ci, c] = value
        ssend[ci] = value.astype(BF16)
        for k in range(1, INQ):
            a, b = place(k)
            send(r1_t[ci][k - 1], ssend.at[ci, a, :, b], r1.at[ci, k - 1], in_quad(k))

    def sum_quad(ci):
        for k in range(1, INQ):
            arrived(r1_t[ci][k - 1], r1.at[ci, k - 1], in_quad(INQ - k))
        value = part[ci, c, pa, :, pb]
        for k in range(INQ - 1):
            value = value + r1[ci, k].astype(F32)
        acc[ci] = value
        arrived(tt[ci], trecv.at[ci], sibling)
        acc[ci, qd] = acc[ci, qd] - trecv[ci].astype(F32)
        a_send[ci] = acc[ci].astype(BF16)
        send(r2_t[ci], a_send.at[ci], r2.at[ci], across)

    def residual(ci):
        arrived(r2_t[ci], r2.at[ci], across)
        errs[ci, c, pa, :, pb] = (acc[ci] + r2[ci].astype(F32)).astype(BF16)
        for k in range(1, INQ):
            send(e2_t[ci][k - 1], errs.at[ci, c, pa, :, pb], errs.at[ci, c, pa, :, pb], in_quad(k))

    def errors_pair(ci):
        for k in range(1, INQ):
            a, b = place(INQ - k)
            arrived(e2_t[ci][k - 1], errs.at[ci, c, a, :, b], in_quad(INQ - k))
        send(es_t[ci], errs.at[ci, c], errs.at[ci, c], sibling)

    def back(ci):
        arrived(es_t[ci], errs.at[ci, 1 - c], sibling)
        value = None
        for u in range(SECT):
            term = jnp.dot(
                errs[ci, u].reshape(CHUNK, HC), pt[u * HC : (u + 1) * HC, :], preferred_element_type=F32
            )
            value = term if value is None else value + term
        value = value.astype(BF16)
        n = 0 if ci in (N1, F1) else 1
        if ci in NEAR:
            gnear[n] = value.reshape(2, NX, TOK, WS)
        else:
            gfar[n] = value.reshape(NY, 2, TOK, WS)
        for to, _, there, here in peers(ci):
            if ci in NEAR:
                send(gnear_t[here], gnear.at[n, to[0] % 2, to[1]], gnear_in.at[there], at(h, *to), gnear_t[0] + there)
            else:
                send(gfar_t[here], gfar.at[n, to[0], to[1] % 2], gfar_in.at[there], at(h, *to), gfar_t[0] + there)

    def collect(value, slots, sems, chunks):
        value = value.astype(F32)
        for ci in chunks:
            for _, of, _, here in peers(ci):
                arrived(sems[here], slots.at[here], at(h, *of))
                value = value + slots[here].astype(F32)
        return value

    def turn(ci):
        ft[ci] = rows_of(ci).T

    done = []

    def grad(ci):
        for u in range(SECT):
            term = jnp.dot(ft[ci], errs[ci, u].reshape(CHUNK, HC), preferred_element_type=F32)
            cols = slice(u * HC, (u + 1) * HC)
            pgrad[:, cols] = term if not done else pgrad[:, cols] + term
        done.append(ci)

    def send_far():
        zsend[...] = collect(gfar[0, y, xb], gfar_in, gfar_t, (F1, F2)).astype(BF16)
        send(z_t, zsend, zrecv, z_mate)

    store_pgrad = pltpu.make_async_copy(pgrad, pgrad_hbm, load_sems.at[5])
    store_igrad = pltpu.make_async_copy(igrad, igrad_hbm, load_sems.at[6])

    far_in()
    predict(N1)
    send_teacher(jnp.logical_not(first_chunk))
    predict(N2)
    sum_pair(N1)
    predict(F1)
    sum_pair(N2)
    turn(N2)
    sum_pair(F1)
    predict(F2)
    sum_quad(N1)
    sum_pair(F2)
    sum_quad(F1)
    sum_quad(F2)
    turn(F1)
    turn(F2)
    residual(F1)
    sum_quad(N2)
    residual(F2)
    errors_pair(F1)
    residual(N1)
    back(F1)
    errors_pair(F2)
    grad(F1)
    residual(N2)
    back(F2)
    errors_pair(N1)
    errors_pair(N2)
    turn(N1)
    back(N1)
    grad(N1)
    send_far()
    back(N2)
    grad(F2)
    grad(N2)
    store_pgrad.start()
    sent.extend(rows_out)

    for op in sent:
        op.wait_send()
    sent.clear()

    feature_grad = collect(gnear[0, yb, x], gnear_in, gnear_t, (N1, N2))
    arrived(z_t, zrecv, z_mate)
    feature_grad = feature_grad + zrecv[...].astype(F32)
    upstream = feature_grad * sg_row

    inner = jnp.sum(upstream * unit, axis=1, keepdims=True)
    stat2[st] = jnp.sum(jnp.where(lanes == rows, inner, zero), axis=0, keepdims=True)
    inner_mean = column(exchange(stat2)(), 0) / DS
    igrad[...] = inv_s * (upstream - unit * inner_mean)
    store_igrad.start()

    for op in sent:
        op.wait_send()
    store_pgrad.wait()
    store_igrad.wait()
    assert used[0] <= SEMS, used


def body(teacher_rows, student_rows, projector, teacher_gain, student_gain):
    anywhere = pl.BlockSpec(memory_space=pl.ANY)
    piece = (2, 2, 2, TOK, HC)
    summed, input_grad = pl.pallas_call(
        kernel,
        out_shape=(
            jax.ShapeDtypeStruct((WS, WC), F32),
            jax.ShapeDtypeStruct((TOK, WS), F32),
        ),
        in_specs=[anywhere] * 5,
        out_specs=(anywhere, anywhere),
        scratch_shapes=[
            pltpu.VMEM((WS, WC), F32),
            pltpu.VMEM((TOK, WS), F32),
            pltpu.VMEM((WC, WS), BF16),
            pltpu.VMEM((4, WS, CHUNK), BF16),
            pltpu.VMEM((TOK, WT), BF16),
            pltpu.VMEM((TOK, WS), BF16),
            pltpu.VMEM((WS, WC), BF16),
            pltpu.VMEM((ST, WT // LANES, LANES), F32),
            pltpu.VMEM((ST, WS // LANES, LANES), F32),
            pltpu.VMEM((ST, 1, LANES), F32),
            pltpu.VMEM((ST, 1, LANES), F32),
            pltpu.VMEM((1, LANES), F32),
            pltpu.VMEM((1, LANES), F32),
            pltpu.VMEM((TOK, WS), BF16),
            pltpu.VMEM((NZH, NY, NX, TOK, WS), BF16),
            pltpu.VMEM((2, SECT, TOK, HC), BF16),
            pltpu.VMEM((4, TOK, HC), BF16),
            pltpu.VMEM((4, SECT) + piece, F32),
            pltpu.VMEM((4,) + piece, F32),
            pltpu.VMEM((4,) + piece, BF16),
            pltpu.VMEM((4, INQ - 1, QUADS, TOK, HC), BF16),
            pltpu.VMEM((4, QUADS, TOK, HC), F32),
            pltpu.VMEM((4, QUADS, TOK, HC), BF16),
            pltpu.VMEM((4, QUADS, TOK, HC), BF16),
            pltpu.VMEM((4, SECT) + piece, BF16),
            pltpu.VMEM((2, 2, NX, TOK, WS), BF16),
            pltpu.VMEM((2, NY, 2, TOK, WS), BF16),
            pltpu.VMEM((15, TOK, WS), BF16),
            pltpu.VMEM((15, TOK, WS), BF16),
            pltpu.VMEM((TOK, WS), BF16),
            pltpu.VMEM((TOK, WS), BF16),
            pltpu.SemaphoreType.DMA((7,)),
            pltpu.SemaphoreType.DMA((SEMS,)),
            pltpu.SemaphoreType.DMA((SEMS,)),
        ],
        compiler_params=pltpu.CompilerParams(
            collective_id=0, has_side_effects=True, vmem_limit_bytes=56 * 1024 * 1024
        ),
    )(
        teacher_rows,
        student_rows,
        projector,
        teacher_gain.reshape(ST, WT // LANES, LANES),
        student_gain.reshape(ST, WS // LANES, LANES),
    )
    return summed * (1.0 / math.sqrt(TOKENS)), input_grad


def solution(mesh):
    return jax.shard_map(
        body,
        mesh=mesh,
        in_specs=(
            P("dp", ("sect", "tensor")),
            P("dp", ("sect", "tensor")),
            P(("sect", "tensor"), "dp"),
            P(),
            P(),
        ),
        out_specs=(P(("sect", "tensor"), "dp"), P("dp", ("sect", "tensor"))),
        check_vma=False,
    )
```

```python
import math

import jax
import jax.numpy as jnp
from jax import lax
from jax.experimental import pallas as pl
from jax.experimental.pallas import tpu as pltpu
from jax.sharding import PartitionSpec as P

epsilon = 1e-05

MESH = pl.DeviceIdType.MESH
DT = 16384
DS = 8192
TOKENS = 1024
SECT = 2
NX = 4
NY = 4
NZH = 2
DP = NZH * NY * NX
QUADS = 2
INQ = 4
TENSOR = QUADS * INQ
ST = SECT * TENSOR
TOK = TOKENS // DP
WT = DT // ST
WS = DS // ST
WC = DT // DP
HC = WC // SECT
CHUNK = TENSOR * TOK
LANES = 128
SEMS = 144
F32 = jnp.float32
BF16 = jnp.bfloat16

N1, F1, F2, N2 = range(4)
NEAR = (N1, N2)


def kernel(
    teacher_hbm, student_hbm, proj_hbm, tgain_hbm, sgain_hbm,
    pgrad_hbm, igrad_hbm,
    pgrad, igrad, pt, ft, teacher, student, proj, tgain, sgain,
    stat, stat2, total_send, total_far, raw_far, feats, tsend, trecv, part, yrecv, ssend, r1, acc, a_send, r2,
    errs, gnear, gfar, gnear_in, gfar_in, zsend, zrecv,
    load_sems, send_sems, recv_sems,
):
    c = lax.axis_index("sect")
    d = lax.axis_index("dp")
    t = lax.axis_index("tensor")
    h, y, x = d // (NY * NX), (d // NX) % NY, d % NX
    qd, zi = t // INQ, t % INQ
    pa, pb = 1 - zi // 2, zi % 2
    st = c * TENSOR + t
    far = 1 - h
    yp, yb, xp, xb = y // 2, y % 2, x // 2, x % 2

    used = [0]
    sent = []

    def tickets(count):
        used[0] += count
        return range(used[0] - count, used[0])

    def dev(sect=None, dp=None, tensor=None):
        return {
            "sect": c if sect is None else sect,
            "dp": d if dp is None else dp,
            "tensor": t if tensor is None else tensor,
        }

    def send(i, src, dst, to, recv=None):
        op = pltpu.make_async_remote_copy(
            src_ref=src, dst_ref=dst, send_sem=send_sems.at[i],
            recv_sem=recv_sems.at[i if recv is None else recv],
            device_id=to, device_id_type=MESH,
        )
        op.start()
        sent.append(op)

    def arrived(i, dst, to):
        pltpu.make_async_remote_copy(
            src_ref=dst, dst_ref=dst, send_sem=send_sems.at[i], recv_sem=recv_sems.at[i],
            device_id=to, device_id_type=MESH,
        ).wait_recv()

    def at(zh, yy, xx):
        return dev(dp=zh * (NY * NX) + yy * NX + xx)

    def x_plus(k):
        return (x + k) % NX

    def y_plus(k):
        return (y + k) % NY

    y_mate, x_mate = y + 1 - 2 * yb, x + 1 - 2 * xb
    z_mate = at(far, y, x)
    sibling = dev(sect=1 - c)
    across = dev(tensor=(1 - qd) * INQ + zi)

    def peers(ci):
        first, out = ci in (N1, F1), []
        for r in range(2):
            for k in range(4):
                if first and r == 0 and k == 0:
                    continue
                if ci in NEAR:
                    line = (y, y_mate)[r] if first else 2 * (1 - yp) + r
                    to, of, mine = (line, x_plus(k)), (line, x_plus(NX - k)), yb
                else:
                    line = (x, x_mate)[r] if first else 2 * (1 - xp) + r
                    to, of, mine = (y_plus(k), line), (y_plus(NY - k), line), xb
                here = 4 * r + k - 1 if first else 7 + 4 * r + k
                there = here if first else 7 + 4 * mine + k
                out.append((to, of, there, here))
        return out

    def in_quad(k):
        return dev(tensor=qd * INQ + (zi + k) % INQ)

    def place(k):
        other = (zi + k) % INQ
        return 1 - other // 2, other % 2

    def st_dev(k):
        other = (st + k) % ST
        return other, dev(sect=other // TENSOR, tensor=other % TENSOR)

    loads = [
        pltpu.make_async_copy(src, dst, load_sems.at[i])
        for i, (src, dst) in enumerate(
            ((student_hbm, student), (teacher_hbm, teacher), (sgain_hbm, sgain), (tgain_hbm, tgain), (proj_hbm, proj))
        )
    ]
    for op in loads:
        op.start()

    barrier = pltpu.get_barrier_semaphore()

    def hello(to):
        pl.semaphore_signal(barrier, inc=1, device_id=to, device_id_type=MESH)

    for k in range(1, ST):
        hello(st_dev(k)[1])
    for k in range(1, NY * NX):
        hello(at(h, y_plus(k // NX), x_plus(k % NX)))
    hello(z_mate)
    source = dict(sect=(d // 2) // TENSOR, tensor=(d // 2) % TENSOR)
    for zh, yy, xx in (
        (h, 2 * yp + pa, 2 * qd + pb),
        (far, 2 * pa + qd, 2 * xp + pb),
        (far, 2 * pa + qd, 2 * (1 - xp) + pb),
        (h, 2 * (1 - yp) + pa, 2 * qd + pb),
    ):
        hello(dev(dp=zh * (NY * NX) + yy * NX + xx, **source))

    rows = lax.broadcasted_iota(jnp.int32, (TOK, LANES), 0)
    lanes = lax.broadcasted_iota(jnp.int32, (TOK, LANES), 1)
    zero = jnp.zeros((TOK, LANES), F32)

    def column(row, first):
        return jnp.sum(jnp.where(lanes == rows + first, row, zero), axis=1, keepdims=True)

    loads[0].wait()
    sf = student[...].astype(F32)
    ssum = jnp.sum(sf * sf, axis=1, keepdims=True)
    loads[1].wait()
    tf = teacher[...].astype(F32)
    tsum = jnp.sum(tf * tf, axis=1, keepdims=True)
    spread = jnp.where(lanes == rows, tsum, zero) + jnp.where(lanes == rows + TOK, ssum, zero)
    stat[st] = jnp.sum(spread, axis=0, keepdims=True)

    pl.semaphore_wait(barrier, (ST - 1) + (NY * NX - 1) + 1 + 4)

    def exchange(ref):
        own = tickets(ST - 1)
        for k in range(1, ST):
            send(own[k - 1], ref.at[st], ref.at[st], st_dev(k)[1])

        def finish():
            for k in range(1, ST):
                other, where = st_dev(ST - k)
                arrived(own[k - 1], ref.at[other], where)
            return jnp.sum(ref[...], axis=0)

        return finish

    finish_stat = exchange(stat)
    raw_t, total_t = tickets(2)
    send(raw_t, student, raw_far, z_mate)

    loads[2].wait()
    sg = sgain[st]
    sg_row = jnp.concatenate([sg[k : k + 1, :] for k in range(WS // LANES)], axis=1)
    loads[3].wait()
    tg = tgain[st]

    loads[4].wait()
    pt[...] = proj[...].T

    total = finish_stat()
    total_send[...] = total
    send(total_t, total_send, total_far, z_mate)
    inv_s = lax.rsqrt(column(total, TOK) / DS + epsilon)
    unit = sf * inv_s
    feats[h, y, x] = (unit * sg_row).astype(BF16)
    near_t, far_t = tickets(15), tickets(15)

    def spread(ci):
        zh, base = (h, near_t[0]) if ci in NEAR else (far, far_t[0])
        for to, _, there, here in peers(ci):
            send(base + here, feats.at[zh, y, x], feats.at[zh, y, x], at(h, *to), base + there)

    spread(N1)
    spread(N2)

    inv_t = lax.rsqrt(column(total, 0) / DT + epsilon)
    for k in range(WT // LANES):
        col = k * LANES
        value = tf[:, col : col + LANES] * inv_t * tg[k : k + 1, :]
        tsend[col // WC, (col % WC) // HC, :, col % HC : col % HC + LANES] = value.astype(BF16)

    tt = tickets(4)
    ts = tickets(4)
    rows_out = []
    near_there = h == c
    to_a = jnp.where(near_there, yb, yp)
    to_q = jnp.where(near_there, xp, yb)
    for j in range(2):
        xp_there = ((2 * t + j) % NX) // 2
        yp_there = t // INQ
        slot = jnp.where(
            near_there,
            jnp.where(yp == yp_there, N1, N2),
            jnp.where(xp == xp_there, F1, F2),
        )
        for u in range(SECT):
            rows_out.append(
                pltpu.make_async_remote_copy(
                    src_ref=tsend.at[j, u], dst_ref=trecv.at[slot],
                    send_sem=send_sems.at[ts[2 * j + u]], recv_sem=recv_sems.at[tt[0] + slot],
                    device_id=dev(sect=u, dp=2 * st + j, tensor=to_q * INQ + (1 - to_a) * 2 + xb),
                    device_id_type=MESH,
                )
            )

    first_chunk = jnp.logical_and(near_there, yp == t // INQ)

    def send_teacher(now):
        @pl.when(now)
        def _():
            for op in rows_out:
                op.start()

    send_teacher(first_chunk)

    def far_in():
        arrived(raw_t, raw_far, z_mate)
        arrived(total_t, total_far, z_mate)
        inv_far = lax.rsqrt(column(total_far[...], TOK) / DS + epsilon)
        feats[far, y, x] = (raw_far[...].astype(F32) * inv_far * sg_row).astype(BF16)
        spread(F1)
        spread(F2)

    def rows_of(ci):
        if ci in NEAR:
            return feats[h, pl.ds(2 * (yp if ci == N1 else 1 - yp), 2)].reshape(CHUNK, WS)
        return feats[far, :, pl.ds(2 * (xp if ci == F1 else 1 - xp), 2)].reshape(CHUNK, WS)

    def features_ready(ci):
        zh, base = (h, near_t[0]) if ci in NEAR else (far, far_t[0])
        for _, of, _, here in peers(ci):
            arrived(base + here, feats.at[zh, of[0], of[1]], at(h, *of))

    pair_t, r1_t, r2_t = tickets(4), [tickets(INQ - 1) for _ in range(4)], tickets(4)
    e2_t, es_t = [tickets(INQ - 1) for _ in range(4)], tickets(4)
    gnear_t, gfar_t = tickets(15), tickets(15)
    (z_t,) = tickets(1)

    def predict(ci):
        features_ready(ci)
        value = rows_of(ci)
        for theirs in (True, False):
            u = 1 - c if theirs else c
            half = jnp.dot(value, proj[:, pl.ds(pl.multiple_of(u * HC, HC), HC)], preferred_element_type=F32)
            part[ci, u] = half.reshape(2, 2, 2, TOK, HC)
            if theirs:
                send(pair_t[ci], part.at[ci, u], yrecv.at[ci], sibling)

    def sum_pair(ci):
        arrived(pair_t[ci], yrecv.at[ci], sibling)
        for k in range(1, INQ):
            a, b = place(k)
            ssend[ci, a, :, b] = (part[ci, c, a, :, b] + yrecv[ci, a, :, b]).astype(BF16)
            send(r1_t[ci][k - 1], ssend.at[ci, a, :, b], r1.at[ci, k - 1], in_quad(k))
        acc[ci] = part[ci, c, pa, :, pb] + yrecv[ci, pa, :, pb]

    def sum_quad(ci):
        value = acc[ci]
        for k in range(1, INQ):
            arrived(r1_t[ci][k - 1], r1.at[ci, k - 1], in_quad(INQ - k))
            value = value + r1[ci, k - 1].astype(F32)
        acc[ci] = value
        arrived(tt[ci], trecv.at[ci], sibling)
        acc[ci, qd] = acc[ci, qd] - trecv[ci].astype(F32)
        a_send[ci] = acc[ci].astype(BF16)
        send(r2_t[ci], a_send.at[ci], r2.at[ci], across)

    def residual(ci):
        arrived(r2_t[ci], r2.at[ci], across)
        errs[ci, c, pa, :, pb] = (acc[ci] + r2[ci].astype(F32)).astype(BF16)
        for k in range(1, INQ):
            send(e2_t[ci][k - 1], errs.at[ci, c, pa, :, pb], errs.at[ci, c, pa, :, pb], in_quad(k))

    def errors_pair(ci):
        for k in range(1, INQ):
            a, b = place(INQ - k)
            arrived(e2_t[ci][k - 1], errs.at[ci, c, a, :, b], in_quad(INQ - k))
        send(es_t[ci], errs.at[ci, c], errs.at[ci, c], sibling)

    def back(ci):
        arrived(es_t[ci], errs.at[ci, 1 - c], sibling)
        n = 0 if ci in (N1, F1) else 1
        for half in range(2):
            value = None
            for u in range(SECT):
                term = jnp.dot(
                    errs[ci, u, half].reshape(CHUNK // 2, HC), pt[u * HC : (u + 1) * HC, :],
                    preferred_element_type=F32,
                )
                value = term if value is None else value + term
            value = value.astype(BF16)
            if ci in NEAR:
                gnear[n, half] = value.reshape(NX, TOK, WS)
            else:
                gfar[n, 2 * half : 2 * half + 2] = value.reshape(2, 2, TOK, WS)
        for to, _, there, here in peers(ci):
            if ci in NEAR:
                send(gnear_t[here], gnear.at[n, to[0] % 2, to[1]], gnear_in.at[there], at(h, *to), gnear_t[0] + there)
            else:
                send(gfar_t[here], gfar.at[n, to[0], to[1] % 2], gfar_in.at[there], at(h, *to), gfar_t[0] + there)

    def collect(value, slots, sems, chunks):
        value = value.astype(F32)
        for ci in chunks:
            for _, of, _, here in peers(ci):
                arrived(sems[here], slots.at[here], at(h, *of))
                value = value + slots[here].astype(F32)
        return value

    def turn(ci):
        ft[ci] = rows_of(ci).T

    done = []

    def grad(ci):
        for u in range(SECT):
            term = jnp.dot(ft[ci], errs[ci, u].reshape(CHUNK, HC), preferred_element_type=F32)
            cols = slice(u * HC, (u + 1) * HC)
            pgrad[:, cols] = term if not done else pgrad[:, cols] + term
        done.append(ci)

    def send_far():
        zsend[...] = collect(gfar[0, y, xb], gfar_in, gfar_t, (F1, F2)).astype(BF16)
        send(z_t, zsend, zrecv, z_mate)

    store_pgrad = pltpu.make_async_copy(pgrad, pgrad_hbm, load_sems.at[5])
    store_igrad = pltpu.make_async_copy(igrad, igrad_hbm, load_sems.at[6])

    far_in()
    predict(N1)
    send_teacher(jnp.logical_not(first_chunk))
    predict(N2)
    sum_pair(N1)
    predict(F1)
    sum_pair(N2)
    turn(N2)
    sum_pair(F1)
    predict(F2)
    sum_quad(N1)
    sum_pair(F2)
    sum_quad(F1)
    sum_quad(F2)
    turn(F1)
    turn(F2)
    residual(F1)
    sum_quad(N2)
    residual(F2)
    errors_pair(F1)
    residual(N1)
    back(F1)
    errors_pair(F2)
    grad(F1)
    residual(N2)
    back(F2)
    errors_pair(N1)
    errors_pair(N2)
    turn(N1)
    back(N1)
    grad(N1)
    send_far()
    back(N2)
    grad(F2)
    grad(N2)
    store_pgrad.start()
    sent.extend(rows_out)

    for op in sent:
        op.wait_send()
    sent.clear()

    feature_grad = collect(gnear[0, yb, x], gnear_in, gnear_t, (N1, N2))
    arrived(z_t, zrecv, z_mate)
    feature_grad = feature_grad + zrecv[...].astype(F32)
    upstream = feature_grad * sg_row

    inner = jnp.sum(upstream * unit, axis=1, keepdims=True)
    stat2[st] = jnp.sum(jnp.where(lanes == rows, inner, zero), axis=0, keepdims=True)
    inner_mean = column(exchange(stat2)(), 0) / DS
    igrad[...] = inv_s * (upstream - unit * inner_mean)
    store_igrad.start()

    for op in sent:
        op.wait_send()
    store_pgrad.wait()
    store_igrad.wait()
    assert used[0] <= SEMS, used


def body(teacher_rows, student_rows, projector, teacher_gain, student_gain):
    anywhere = pl.BlockSpec(memory_space=pl.ANY)
    piece = (2, 2, 2, TOK, HC)
    summed, input_grad = pl.pallas_call(
        kernel,
        out_shape=(
            jax.ShapeDtypeStruct((WS, WC), F32),
            jax.ShapeDtypeStruct((TOK, WS), F32),
        ),
        in_specs=[anywhere] * 5,
        out_specs=(anywhere, anywhere),
        scratch_shapes=[
            pltpu.VMEM((WS, WC), F32),
            pltpu.VMEM((TOK, WS), F32),
            pltpu.VMEM((WC, WS), BF16),
            pltpu.VMEM((4, WS, CHUNK), BF16),
            pltpu.VMEM((TOK, WT), BF16),
            pltpu.VMEM((TOK, WS), BF16),
            pltpu.VMEM((WS, WC), BF16),
            pltpu.VMEM((ST, WT // LANES, LANES), F32),
            pltpu.VMEM((ST, WS // LANES, LANES), F32),
            pltpu.VMEM((ST, 1, LANES), F32),
            pltpu.VMEM((ST, 1, LANES), F32),
            pltpu.VMEM((1, LANES), F32),
            pltpu.VMEM((1, LANES), F32),
            pltpu.VMEM((TOK, WS), BF16),
            pltpu.VMEM((NZH, NY, NX, TOK, WS), BF16),
            pltpu.VMEM((2, SECT, TOK, HC), BF16),
            pltpu.VMEM((4, TOK, HC), BF16),
            pltpu.VMEM((4, SECT) + piece, F32),
            pltpu.VMEM((4,) + piece, F32),
            pltpu.VMEM((4,) + piece, BF16),
            pltpu.VMEM((4, INQ - 1, QUADS, TOK, HC), BF16),
            pltpu.VMEM((4, QUADS, TOK, HC), F32),
            pltpu.VMEM((4, QUADS, TOK, HC), BF16),
            pltpu.VMEM((4, QUADS, TOK, HC), BF16),
            pltpu.VMEM((4, SECT) + piece, BF16),
            pltpu.VMEM((2, 2, NX, TOK, WS), BF16),
            pltpu.VMEM((2, NY, 2, TOK, WS), BF16),
            pltpu.VMEM((15, TOK, WS), BF16),
            pltpu.VMEM((15, TOK, WS), BF16),
            pltpu.VMEM((TOK, WS), BF16),
            pltpu.VMEM((TOK, WS), BF16),
            pltpu.SemaphoreType.DMA((7,)),
            pltpu.SemaphoreType.DMA((SEMS,)),
            pltpu.SemaphoreType.DMA((SEMS,)),
        ],
        compiler_params=pltpu.CompilerParams(
            collective_id=0, has_side_effects=True, vmem_limit_bytes=56 * 1024 * 1024
        ),
    )(
        teacher_rows,
        student_rows,
        projector,
        teacher_gain.reshape(ST, WT // LANES, LANES),
        student_gain.reshape(ST, WS // LANES, LANES),
    )
    return summed * (1.0 / math.sqrt(TOKENS)), input_grad


def solution(mesh):
    return jax.shard_map(
        body,
        mesh=mesh,
        in_specs=(
            P("dp", ("sect", "tensor")),
            P("dp", ("sect", "tensor")),
            P(("sect", "tensor"), "dp"),
            P(),
            P(),
        ),
        out_specs=(P(("sect", "tensor"), "dp"), P("dp", ("sect", "tensor"))),
        check_vma=False,
    )
```

```python
import math

import jax
import jax.numpy as jnp
from jax import lax
from jax.experimental import pallas as pl
from jax.experimental.pallas import tpu as pltpu
from jax.sharding import PartitionSpec as P

epsilon = 1e-05

MESH = pl.DeviceIdType.MESH
DT = 16384
DS = 8192
TOKENS = 1024
SECT = 2
NX = 4
NY = 4
NZH = 2
DP = NZH * NY * NX
QUADS = 2
INQ = 4
TENSOR = QUADS * INQ
ST = SECT * TENSOR
TOK = TOKENS // DP
WT = DT // ST
WS = DS // ST
WC = DT // DP
HC = WC // SECT
CHUNK = TENSOR * TOK
LANES = 128
SEMS = 144
STORES = 8
F32 = jnp.float32
BF16 = jnp.bfloat16

N1, F1, F2, N2 = range(4)
NEAR = (N1, N2)


def kernel(
    teacher_hbm, student_hbm, proj_hbm, tgain_hbm, sgain_hbm,
    pgrad_hbm, igrad_hbm,
    pgrad, igrad, pt, ft, teacher, student, proj, tgain, sgain,
    stat, stat2, total_send, total_far, raw_far, feats, tsend, trecv, part, yrecv, ssend, r1, acc, a_send, r2,
    errs, gnear, gfar, gnear_in, gfar_in, zsend, zrecv,
    load_sems, send_sems, recv_sems,
):
    c = lax.axis_index("sect")
    d = lax.axis_index("dp")
    t = lax.axis_index("tensor")
    h, y, x = d // (NY * NX), (d // NX) % NY, d % NX
    qd, zi = t // INQ, t % INQ
    pa, pb = 1 - zi // 2, zi % 2
    st = c * TENSOR + t
    far = 1 - h
    yp, yb, xp, xb = y // 2, y % 2, x // 2, x % 2

    used = [0]
    sent = []

    def tickets(count):
        used[0] += count
        return range(used[0] - count, used[0])

    def dev(sect=None, dp=None, tensor=None):
        return {
            "sect": c if sect is None else sect,
            "dp": d if dp is None else dp,
            "tensor": t if tensor is None else tensor,
        }

    def send(i, src, dst, to, recv=None):
        op = pltpu.make_async_remote_copy(
            src_ref=src, dst_ref=dst, send_sem=send_sems.at[i],
            recv_sem=recv_sems.at[i if recv is None else recv],
            device_id=to, device_id_type=MESH,
        )
        op.start()
        sent.append(op)

    def arrived(i, dst, to):
        pltpu.make_async_remote_copy(
            src_ref=dst, dst_ref=dst, send_sem=send_sems.at[i], recv_sem=recv_sems.at[i],
            device_id=to, device_id_type=MESH,
        ).wait_recv()

    def at(zh, yy, xx):
        return dev(dp=zh * (NY * NX) + yy * NX + xx)

    def x_plus(k):
        return (x + k) % NX

    def y_plus(k):
        return (y + k) % NY

    y_mate, x_mate = y + 1 - 2 * yb, x + 1 - 2 * xb
    z_mate = at(far, y, x)
    sibling = dev(sect=1 - c)
    across = dev(tensor=(1 - qd) * INQ + zi)

    def peers(ci):
        first, out = ci in (N1, F1), []
        for r in range(2):
            for k in range(4):
                if first and r == 0 and k == 0:
                    continue
                if ci in NEAR:
                    line = (y, y_mate)[r] if first else 2 * (1 - yp) + r
                    to, of, mine = (line, x_plus(k)), (line, x_plus(NX - k)), yb
                else:
                    line = (x, x_mate)[r] if first else 2 * (1 - xp) + r
                    to, of, mine = (y_plus(k), line), (y_plus(NY - k), line), xb
                here = 4 * r + k - 1 if first else 7 + 4 * r + k
                there = here if first else 7 + 4 * mine + k
                out.append((to, of, there, here))
        return out

    def in_quad(k):
        return dev(tensor=qd * INQ + (zi + k) % INQ)

    def place(k):
        other = (zi + k) % INQ
        return 1 - other // 2, other % 2

    def st_dev(k):
        other = (st + k) % ST
        return other, dev(sect=other // TENSOR, tensor=other % TENSOR)

    loads = [
        pltpu.make_async_copy(src, dst, load_sems.at[i])
        for i, (src, dst) in enumerate(
            ((student_hbm, student), (teacher_hbm, teacher), (sgain_hbm, sgain), (tgain_hbm, tgain), (proj_hbm, proj))
        )
    ]
    for op in loads:
        op.start()

    barrier = pltpu.get_barrier_semaphore()

    def hello(to):
        pl.semaphore_signal(barrier, inc=1, device_id=to, device_id_type=MESH)

    for k in range(1, ST):
        hello(st_dev(k)[1])
    for k in range(1, NY * NX):
        hello(at(h, y_plus(k // NX), x_plus(k % NX)))
    hello(z_mate)
    source = dict(sect=(d // 2) // TENSOR, tensor=(d // 2) % TENSOR)
    for zh, yy, xx in (
        (h, 2 * yp + pa, 2 * qd + pb),
        (far, 2 * pa + qd, 2 * xp + pb),
        (far, 2 * pa + qd, 2 * (1 - xp) + pb),
        (h, 2 * (1 - yp) + pa, 2 * qd + pb),
    ):
        hello(dev(dp=zh * (NY * NX) + yy * NX + xx, **source))

    rows = lax.broadcasted_iota(jnp.int32, (TOK, LANES), 0)
    lanes = lax.broadcasted_iota(jnp.int32, (TOK, LANES), 1)
    zero = jnp.zeros((TOK, LANES), F32)

    def column(row, first):
        return jnp.sum(jnp.where(lanes == rows + first, row, zero), axis=1, keepdims=True)

    loads[0].wait()
    sf = student[...].astype(F32)
    ssum = jnp.sum(sf * sf, axis=1, keepdims=True)
    loads[1].wait()
    tf = teacher[...].astype(F32)
    tsum = jnp.sum(tf * tf, axis=1, keepdims=True)
    spread = jnp.where(lanes == rows, tsum, zero) + jnp.where(lanes == rows + TOK, ssum, zero)
    stat[st] = jnp.sum(spread, axis=0, keepdims=True)

    pl.semaphore_wait(barrier, (ST - 1) + (NY * NX - 1) + 1 + 4)

    def exchange(ref):
        own = tickets(ST - 1)
        for k in range(1, ST):
            send(own[k - 1], ref.at[st], ref.at[st], st_dev(k)[1])

        def finish():
            for k in range(1, ST):
                other, where = st_dev(ST - k)
                arrived(own[k - 1], ref.at[other], where)
            return jnp.sum(ref[...], axis=0)

        return finish

    finish_stat = exchange(stat)
    raw_t, total_t = tickets(2)
    send(raw_t, student, raw_far, z_mate)

    loads[2].wait()
    sg = sgain[st]
    sg_row = jnp.concatenate([sg[k : k + 1, :] for k in range(WS // LANES)], axis=1)
    loads[3].wait()
    tg = tgain[st]

    loads[4].wait()
    pt[...] = proj[...].T

    total = finish_stat()
    total_send[...] = total
    send(total_t, total_send, total_far, z_mate)
    inv_s = lax.rsqrt(column(total, TOK) / DS + epsilon)
    unit = sf * inv_s
    feats[h, y, x] = (unit * sg_row).astype(BF16)
    near_t, far_t = tickets(15), tickets(15)

    def spread(ci):
        zh, base = (h, near_t[0]) if ci in NEAR else (far, far_t[0])
        for to, _, there, here in peers(ci):
            send(base + here, feats.at[zh, y, x], feats.at[zh, y, x], at(h, *to), base + there)

    spread(N1)
    spread(N2)

    inv_t = lax.rsqrt(column(total, 0) / DT + epsilon)
    for k in range(WT // LANES):
        col = k * LANES
        value = tf[:, col : col + LANES] * inv_t * tg[k : k + 1, :]
        tsend[col // WC, (col % WC) // HC, :, col % HC : col % HC + LANES] = value.astype(BF16)

    tt = tickets(4)
    ts = tickets(4)
    rows_out = []
    near_there = h == c
    to_a = jnp.where(near_there, yb, yp)
    to_q = jnp.where(near_there, xp, yb)
    for j in range(2):
        xp_there = ((2 * t + j) % NX) // 2
        yp_there = t // INQ
        slot = jnp.where(
            near_there,
            jnp.where(yp == yp_there, N1, N2),
            jnp.where(xp == xp_there, F1, F2),
        )
        for u in range(SECT):
            rows_out.append(
                pltpu.make_async_remote_copy(
                    src_ref=tsend.at[j, u], dst_ref=trecv.at[slot],
                    send_sem=send_sems.at[ts[2 * j + u]], recv_sem=recv_sems.at[tt[0] + slot],
                    device_id=dev(sect=u, dp=2 * st + j, tensor=to_q * INQ + (1 - to_a) * 2 + xb),
                    device_id_type=MESH,
                )
            )

    first_chunk = jnp.logical_and(near_there, yp == t // INQ)

    def send_teacher(now):
        @pl.when(now)
        def _():
            for op in rows_out:
                op.start()

    send_teacher(first_chunk)

    def far_in():
        arrived(raw_t, raw_far, z_mate)
        arrived(total_t, total_far, z_mate)
        inv_far = lax.rsqrt(column(total_far[...], TOK) / DS + epsilon)
        feats[far, y, x] = (raw_far[...].astype(F32) * inv_far * sg_row).astype(BF16)
        spread(F1)
        spread(F2)

    def rows_of(ci):
        if ci in NEAR:
            return feats[h, pl.ds(2 * (yp if ci == N1 else 1 - yp), 2)].reshape(CHUNK, WS)
        return feats[far, :, pl.ds(2 * (xp if ci == F1 else 1 - xp), 2)].reshape(CHUNK, WS)

    def features_ready(ci):
        zh, base = (h, near_t[0]) if ci in NEAR else (far, far_t[0])
        for _, of, _, here in peers(ci):
            arrived(base + here, feats.at[zh, of[0], of[1]], at(h, *of))

    pair_t, r1_t, r2_t = tickets(4), [tickets(INQ - 1) for _ in range(4)], tickets(4)
    e2_t, es_t = [tickets(INQ - 1) for _ in range(4)], tickets(4)
    gnear_t, gfar_t = tickets(15), tickets(15)
    (z_t,) = tickets(1)

    def predict(ci):
        features_ready(ci)
        value = rows_of(ci)
        for theirs in (True, False):
            u = 1 - c if theirs else c
            half = jnp.dot(value, proj[:, pl.ds(pl.multiple_of(u * HC, HC), HC)], preferred_element_type=F32)
            part[ci, u] = half.reshape(2, 2, 2, TOK, HC)
            if theirs:
                send(pair_t[ci], part.at[ci, u], yrecv.at[ci], sibling)

    def sum_pair(ci):
        arrived(pair_t[ci], yrecv.at[ci], sibling)
        for k in range(1, INQ):
            a, b = place(k)
            ssend[ci, a, :, b] = (part[ci, c, a, :, b] + yrecv[ci, a, :, b]).astype(BF16)
            send(r1_t[ci][k - 1], ssend.at[ci, a, :, b], r1.at[ci, k - 1], in_quad(k))
        acc[ci] = part[ci, c, pa, :, pb] + yrecv[ci, pa, :, pb]

    def sum_quad(ci):
        value = acc[ci]
        for k in range(1, INQ):
            arrived(r1_t[ci][k - 1], r1.at[ci, k - 1], in_quad(INQ - k))
            value = value + r1[ci, k - 1].astype(F32)
        acc[ci] = value
        arrived(tt[ci], trecv.at[ci], sibling)
        acc[ci, qd] = acc[ci, qd] - trecv[ci].astype(F32)
        a_send[ci] = acc[ci].astype(BF16)
        send(r2_t[ci], a_send.at[ci], r2.at[ci], across)

    def residual(ci):
        arrived(r2_t[ci], r2.at[ci], across)
        errs[ci, c, pa, :, pb] = (acc[ci] + r2[ci].astype(F32)).astype(BF16)
        for k in range(1, INQ):
            send(e2_t[ci][k - 1], errs.at[ci, c, pa, :, pb], errs.at[ci, c, pa, :, pb], in_quad(k))

    def errors_pair(ci):
        for k in range(1, INQ):
            a, b = place(INQ - k)
            arrived(e2_t[ci][k - 1], errs.at[ci, c, a, :, b], in_quad(INQ - k))
        send(es_t[ci], errs.at[ci, c], errs.at[ci, c], sibling)

    def back(ci):
        arrived(es_t[ci], errs.at[ci, 1 - c], sibling)
        n = 0 if ci in (N1, F1) else 1
        for half in range(2):
            value = None
            for u in range(SECT):
                term = jnp.dot(
                    errs[ci, u, half].reshape(CHUNK // 2, HC), pt[u * HC : (u + 1) * HC, :],
                    preferred_element_type=F32,
                )
                value = term if value is None else value + term
            value = value.astype(BF16)
            if ci in NEAR:
                gnear[n, half] = value.reshape(NX, TOK, WS)
            else:
                gfar[n, 2 * half : 2 * half + 2] = value.reshape(2, 2, TOK, WS)
        for to, _, there, here in peers(ci):
            if ci in NEAR:
                send(gnear_t[here], gnear.at[n, to[0] % 2, to[1]], gnear_in.at[there], at(h, *to), gnear_t[0] + there)
            else:
                send(gfar_t[here], gfar.at[n, to[0], to[1] % 2], gfar_in.at[there], at(h, *to), gfar_t[0] + there)

    def collect(value, slots, sems, chunks):
        value = value.astype(F32)
        for ci in chunks:
            for _, of, _, here in peers(ci):
                arrived(sems[here], slots.at[here], at(h, *of))
                value = value + slots[here].astype(F32)
        return value

    def turn(ci):
        ft[ci] = rows_of(ci).T

    done = []

    def grad(ci):
        for u in range(SECT):
            term = jnp.dot(ft[ci], errs[ci, u].reshape(CHUNK, HC), preferred_element_type=F32)
            cols = slice(u * HC, (u + 1) * HC)
            if done:
                term = pgrad[:, cols] + term
            pgrad[:, cols] = term * (1.0 / math.sqrt(TOKENS)) if len(done) == 3 else term
        done.append(ci)

    def send_far():
        zsend[...] = collect(gfar[0, y, xb], gfar_in, gfar_t, (F1, F2)).astype(BF16)
        send(z_t, zsend, zrecv, z_mate)

    store_pgrad = pltpu.make_async_copy(pgrad, pgrad_hbm, load_sems.at[5])
    store_igrad = pltpu.make_async_copy(igrad, igrad_hbm, load_sems.at[6])

    far_in()
    predict(N1)
    send_teacher(jnp.logical_not(first_chunk))
    predict(N2)
    sum_pair(N1)
    predict(F1)
    sum_pair(N2)
    turn(N2)
    sum_pair(F1)
    predict(F2)
    sum_quad(N1)
    sum_pair(F2)
    sum_quad(F1)
    sum_quad(F2)
    turn(F1)
    turn(F2)
    residual(F1)
    sum_quad(N2)
    residual(F2)
    errors_pair(F1)
    residual(N1)
    back(F1)
    errors_pair(F2)
    grad(F1)
    residual(N2)
    back(F2)
    errors_pair(N1)
    errors_pair(N2)
    turn(N1)
    back(N1)
    grad(N1)
    send_far()
    back(N2)
    grad(F2)
    grad(N2)
    store_pgrad.start()
    sent.extend(rows_out)

    for op in sent:
        op.wait_send()
    sent.clear()

    feature_grad = collect(gnear[0, yb, x], gnear_in, gnear_t, (N1, N2))
    arrived(z_t, zrecv, z_mate)
    feature_grad = feature_grad + zrecv[...].astype(F32)
    upstream = feature_grad * sg_row

    inner = jnp.sum(upstream * unit, axis=1, keepdims=True)
    stat2[st] = jnp.sum(jnp.where(lanes == rows, inner, zero), axis=0, keepdims=True)
    inner_mean = column(exchange(stat2)(), 0) / DS
    igrad[...] = inv_s * (upstream - unit * inner_mean)
    store_igrad.start()

    for op in sent:
        op.wait_send()
    store_pgrad.wait()
    store_igrad.wait()
    assert used[0] <= SEMS, used


def store(pgrad_in, igrad_in, pgrad_out, igrad_out, sems):
    step = WS // STORES
    ops = [pltpu.make_async_copy(igrad_in, igrad_out, sems.at[STORES])]
    for i in range(STORES):
        rows = pl.ds(i * step, step)
        ops.append(pltpu.make_async_copy(pgrad_in.at[rows], pgrad_out.at[rows], sems.at[i]))
    for op in ops:
        op.start()
    for op in ops:
        op.wait()


def body(teacher_rows, student_rows, projector, teacher_gain, student_gain):
    anywhere = pl.BlockSpec(memory_space=pl.ANY)
    piece = (2, 2, 2, TOK, HC)
    results = pl.pallas_call(
        kernel,
        out_shape=(
            jax.ShapeDtypeStruct((WS, WC), F32),
            jax.ShapeDtypeStruct((TOK, WS), F32),
        ),
        in_specs=[anywhere] * 5,
        out_specs=(anywhere, anywhere),
        scratch_shapes=[
            pltpu.VMEM((WS, WC), F32),
            pltpu.VMEM((TOK, WS), F32),
            pltpu.VMEM((WC, WS), BF16),
            pltpu.VMEM((4, WS, CHUNK), BF16),
            pltpu.VMEM((TOK, WT), BF16),
            pltpu.VMEM((TOK, WS), BF16),
            pltpu.VMEM((WS, WC), BF16),
            pltpu.VMEM((ST, WT // LANES, LANES), F32),
            pltpu.VMEM((ST, WS // LANES, LANES), F32),
            pltpu.VMEM((ST, 1, LANES), F32),
            pltpu.VMEM((ST, 1, LANES), F32),
            pltpu.VMEM((1, LANES), F32),
            pltpu.VMEM((1, LANES), F32),
            pltpu.VMEM((TOK, WS), BF16),
            pltpu.VMEM((NZH, NY, NX, TOK, WS), BF16),
            pltpu.VMEM((2, SECT, TOK, HC), BF16),
            pltpu.VMEM((4, TOK, HC), BF16),
            pltpu.VMEM((4, SECT) + piece, F32),
            pltpu.VMEM((4,) + piece, F32),
            pltpu.VMEM((4,) + piece, BF16),
            pltpu.VMEM((4, INQ - 1, QUADS, TOK, HC), BF16),
            pltpu.VMEM((4, QUADS, TOK, HC), F32),
            pltpu.VMEM((4, QUADS, TOK, HC), BF16),
            pltpu.VMEM((4, QUADS, TOK, HC), BF16),
            pltpu.VMEM((4, SECT) + piece, BF16),
            pltpu.VMEM((2, 2, NX, TOK, WS), BF16),
            pltpu.VMEM((2, NY, 2, TOK, WS), BF16),
            pltpu.VMEM((15, TOK, WS), BF16),
            pltpu.VMEM((15, TOK, WS), BF16),
            pltpu.VMEM((TOK, WS), BF16),
            pltpu.VMEM((TOK, WS), BF16),
            pltpu.SemaphoreType.DMA((7,)),
            pltpu.SemaphoreType.DMA((SEMS,)),
            pltpu.SemaphoreType.DMA((SEMS,)),
        ],
        compiler_params=pltpu.CompilerParams(
            collective_id=0, has_side_effects=True, vmem_limit_bytes=56 * 1024 * 1024
        ),
    )(
        teacher_rows,
        student_rows,
        projector,
        teacher_gain.reshape(ST, WT // LANES, LANES),
        student_gain.reshape(ST, WS // LANES, LANES),
    )
    return pl.pallas_call(
        store,
        out_shape=(
            jax.ShapeDtypeStruct((WS, WC), F32),
            jax.ShapeDtypeStruct((TOK, WS), F32),
        ),
        in_specs=[anywhere] * 2,
        out_specs=(anywhere, anywhere),
        scratch_shapes=[pltpu.SemaphoreType.DMA((STORES + 1,))],
        compiler_params=pltpu.CompilerParams(vmem_limit_bytes=60 * 1024 * 1024),
    )(*results)


def solution(mesh):
    return jax.shard_map(
        body,
        mesh=mesh,
        in_specs=(
            P("dp", ("sect", "tensor")),
            P("dp", ("sect", "tensor")),
            P(("sect", "tensor"), "dp"),
            P(),
            P(),
        ),
        out_specs=(P(("sect", "tensor"), "dp"), P("dp", ("sect", "tensor"))),
        check_vma=False,
    )
```

```python
import math

import jax
import jax.numpy as jnp
from jax import lax
from jax.experimental import pallas as pl
from jax.experimental.pallas import tpu as pltpu
from jax.sharding import PartitionSpec as P

epsilon = 1e-05

MESH = pl.DeviceIdType.MESH
DT = 16384
DS = 8192
TOKENS = 1024
SECT = 2
NX = 4
NY = 4
NZH = 2
DP = NZH * NY * NX
QUADS = 2
INQ = 4
TENSOR = QUADS * INQ
ST = SECT * TENSOR
TOK = TOKENS // DP
WT = DT // ST
WS = DS // ST
WC = DT // DP
HC = WC // SECT
CHUNK = TENSOR * TOK
LANES = 128
SEMS = 144
STORES = 4
F32 = jnp.float32
BF16 = jnp.bfloat16

N1, F1, F2, N2 = range(4)
NEAR = (N1, N2)


def kernel(
    teacher_hbm, student_hbm, proj_hbm, tgain_hbm, sgain_hbm,
    pgrad_hbm, igrad_hbm,
    pgrad, igrad, pt, ft, teacher, student, proj, tgain, sgain,
    stat, stat2, total_send, total_far, raw_far, feats, tsend, trecv, part, yrecv, ssend, r1, acc, a_send, r2,
    errs, gnear, gfar, gnear_in, gfar_in, zsend, zrecv,
    load_sems, send_sems, recv_sems,
):
    c = lax.axis_index("sect")
    d = lax.axis_index("dp")
    t = lax.axis_index("tensor")
    h, y, x = d // (NY * NX), (d // NX) % NY, d % NX
    qd, zi = t // INQ, t % INQ
    pa, pb = 1 - zi // 2, zi % 2
    st = c * TENSOR + t
    far = 1 - h
    yp, yb, xp, xb = y // 2, y % 2, x // 2, x % 2

    used = [0]
    sent = []

    def tickets(count):
        used[0] += count
        return range(used[0] - count, used[0])

    def dev(sect=None, dp=None, tensor=None):
        return {
            "sect": c if sect is None else sect,
            "dp": d if dp is None else dp,
            "tensor": t if tensor is None else tensor,
        }

    def send(i, src, dst, to, recv=None):
        op = pltpu.make_async_remote_copy(
            src_ref=src, dst_ref=dst, send_sem=send_sems.at[i],
            recv_sem=recv_sems.at[i if recv is None else recv],
            device_id=to, device_id_type=MESH,
        )
        op.start()
        sent.append(op)

    def arrived(i, dst, to):
        pltpu.make_async_remote_copy(
            src_ref=dst, dst_ref=dst, send_sem=send_sems.at[i], recv_sem=recv_sems.at[i],
            device_id=to, device_id_type=MESH,
        ).wait_recv()

    def at(zh, yy, xx):
        return dev(dp=zh * (NY * NX) + yy * NX + xx)

    def x_plus(k):
        return (x + k) % NX

    def y_plus(k):
        return (y + k) % NY

    y_mate, x_mate = y + 1 - 2 * yb, x + 1 - 2 * xb
    z_mate = at(far, y, x)
    sibling = dev(sect=1 - c)
    across = dev(tensor=(1 - qd) * INQ + zi)

    def peers(ci):
        first, out = ci in (N1, F1), []
        for r in range(2):
            for k in range(4):
                if first and r == 0 and k == 0:
                    continue
                if ci in NEAR:
                    line = (y, y_mate)[r] if first else 2 * (1 - yp) + r
                    to, of, mine = (line, x_plus(k)), (line, x_plus(NX - k)), yb
                else:
                    line = (x, x_mate)[r] if first else 2 * (1 - xp) + r
                    to, of, mine = (y_plus(k), line), (y_plus(NY - k), line), xb
                here = 4 * r + k - 1 if first else 7 + 4 * r + k
                there = here if first else 7 + 4 * mine + k
                out.append((to, of, there, here))
        return out

    def in_quad(k):
        return dev(tensor=qd * INQ + (zi + k) % INQ)

    def place(k):
        other = (zi + k) % INQ
        return 1 - other // 2, other % 2

    def st_dev(k):
        other = (st + k) % ST
        return other, dev(sect=other // TENSOR, tensor=other % TENSOR)

    loads = [
        pltpu.make_async_copy(src, dst, load_sems.at[i])
        for i, (src, dst) in enumerate(
            ((student_hbm, student), (teacher_hbm, teacher), (sgain_hbm, sgain), (tgain_hbm, tgain), (proj_hbm, proj))
        )
    ]
    for op in loads:
        op.start()

    barrier = pltpu.get_barrier_semaphore()

    def hello(to):
        pl.semaphore_signal(barrier, inc=1, device_id=to, device_id_type=MESH)

    for k in range(1, ST):
        hello(st_dev(k)[1])
    for k in range(1, NY * NX):
        hello(at(h, y_plus(k // NX), x_plus(k % NX)))
    hello(z_mate)
    source = dict(sect=(d // 2) // TENSOR, tensor=(d // 2) % TENSOR)
    for zh, yy, xx in (
        (h, 2 * yp + pa, 2 * qd + pb),
        (far, 2 * pa + qd, 2 * xp + pb),
        (far, 2 * pa + qd, 2 * (1 - xp) + pb),
        (h, 2 * (1 - yp) + pa, 2 * qd + pb),
    ):
        hello(dev(dp=zh * (NY * NX) + yy * NX + xx, **source))

    rows = lax.broadcasted_iota(jnp.int32, (TOK, LANES), 0)
    lanes = lax.broadcasted_iota(jnp.int32, (TOK, LANES), 1)
    zero = jnp.zeros((TOK, LANES), F32)

    def column(row, first):
        return jnp.sum(jnp.where(lanes == rows + first, row, zero), axis=1, keepdims=True)

    loads[0].wait()
    sf = student[...].astype(F32)
    ssum = jnp.sum(sf * sf, axis=1, keepdims=True)
    loads[1].wait()
    tf = teacher[...].astype(F32)
    tsum = jnp.sum(tf * tf, axis=1, keepdims=True)
    spread = jnp.where(lanes == rows, tsum, zero) + jnp.where(lanes == rows + TOK, ssum, zero)
    stat[st] = jnp.sum(spread, axis=0, keepdims=True)

    pl.semaphore_wait(barrier, (ST - 1) + (NY * NX - 1) + 1 + 4)

    def exchange(ref):
        own = tickets(ST - 1)
        for k in range(1, ST):
            send(own[k - 1], ref.at[st], ref.at[st], st_dev(k)[1])

        def finish():
            for k in range(1, ST):
                other, where = st_dev(ST - k)
                arrived(own[k - 1], ref.at[other], where)
            return jnp.sum(ref[...], axis=0)

        return finish

    finish_stat = exchange(stat)
    raw_t, total_t = tickets(2)
    send(raw_t, student, raw_far, z_mate)

    loads[2].wait()
    sg = sgain[st]
    sg_row = jnp.concatenate([sg[k : k + 1, :] for k in range(WS // LANES)], axis=1)
    loads[3].wait()
    tg = tgain[st]

    loads[4].wait()
    pt[...] = proj[...].T

    total = finish_stat()
    total_send[...] = total
    send(total_t, total_send, total_far, z_mate)
    inv_s = lax.rsqrt(column(total, TOK) / DS + epsilon)
    unit = sf * inv_s
    feats[h, y, x] = (unit * sg_row).astype(BF16)
    near_t, far_t = tickets(15), tickets(15)

    def spread(ci):
        zh, base = (h, near_t[0]) if ci in NEAR else (far, far_t[0])
        for to, _, there, here in peers(ci):
            send(base + here, feats.at[zh, y, x], feats.at[zh, y, x], at(h, *to), base + there)

    spread(N1)
    spread(N2)

    inv_t = lax.rsqrt(column(total, 0) / DT + epsilon)
    for k in range(WT // LANES):
        col = k * LANES
        value = tf[:, col : col + LANES] * inv_t * tg[k : k + 1, :]
        tsend[col // WC, (col % WC) // HC, :, col % HC : col % HC + LANES] = value.astype(BF16)

    tt = tickets(4)
    ts = tickets(4)
    rows_out = []
    near_there = h == c
    to_a = jnp.where(near_there, yb, yp)
    to_q = jnp.where(near_there, xp, yb)
    for j in range(2):
        xp_there = ((2 * t + j) % NX) // 2
        yp_there = t // INQ
        slot = jnp.where(
            near_there,
            jnp.where(yp == yp_there, N1, N2),
            jnp.where(xp == xp_there, F1, F2),
        )
        for u in range(SECT):
            rows_out.append(
                pltpu.make_async_remote_copy(
                    src_ref=tsend.at[j, u], dst_ref=trecv.at[slot],
                    send_sem=send_sems.at[ts[2 * j + u]], recv_sem=recv_sems.at[tt[0] + slot],
                    device_id=dev(sect=u, dp=2 * st + j, tensor=to_q * INQ + (1 - to_a) * 2 + xb),
                    device_id_type=MESH,
                )
            )

    first_chunk = jnp.logical_and(near_there, yp == t // INQ)

    def send_teacher(now):
        @pl.when(now)
        def _():
            for op in rows_out:
                op.start()

    send_teacher(first_chunk)

    def far_in():
        arrived(raw_t, raw_far, z_mate)
        arrived(total_t, total_far, z_mate)
        inv_far = lax.rsqrt(column(total_far[...], TOK) / DS + epsilon)
        feats[far, y, x] = (raw_far[...].astype(F32) * inv_far * sg_row).astype(BF16)
        spread(F1)
        spread(F2)

    def rows_of(ci):
        if ci in NEAR:
            return feats[h, pl.ds(2 * (yp if ci == N1 else 1 - yp), 2)].reshape(CHUNK, WS)
        return feats[far, :, pl.ds(2 * (xp if ci == F1 else 1 - xp), 2)].reshape(CHUNK, WS)

    def features_ready(ci):
        zh, base = (h, near_t[0]) if ci in NEAR else (far, far_t[0])
        for _, of, _, here in peers(ci):
            arrived(base + here, feats.at[zh, of[0], of[1]], at(h, *of))

    pair_t, r1_t, r2_t = tickets(4), [tickets(INQ - 1) for _ in range(4)], tickets(4)
    e2_t, es_t = [tickets(INQ - 1) for _ in range(4)], tickets(4)
    gnear_t, gfar_t = tickets(15), tickets(15)
    (z_t,) = tickets(1)

    def predict(ci):
        features_ready(ci)
        value = rows_of(ci)
        for theirs in (True, False):
            u = 1 - c if theirs else c
            half = jnp.dot(value, proj[:, pl.ds(pl.multiple_of(u * HC, HC), HC)], preferred_element_type=F32)
            part[ci, u] = half.reshape(2, 2, 2, TOK, HC)
            if theirs:
                send(pair_t[ci], part.at[ci, u], yrecv.at[ci], sibling)

    def sum_pair(ci):
        arrived(pair_t[ci], yrecv.at[ci], sibling)
        for k in range(1, INQ):
            a, b = place(k)
            ssend[ci, a, :, b] = (part[ci, c, a, :, b] + yrecv[ci, a, :, b]).astype(BF16)
            send(r1_t[ci][k - 1], ssend.at[ci, a, :, b], r1.at[ci, k - 1], in_quad(k))
        acc[ci] = part[ci, c, pa, :, pb] + yrecv[ci, pa, :, pb]

    def sum_quad(ci):
        value = acc[ci]
        for k in range(1, INQ):
            arrived(r1_t[ci][k - 1], r1.at[ci, k - 1], in_quad(INQ - k))
            value = value + r1[ci, k - 1].astype(F32)
        acc[ci] = value
        arrived(tt[ci], trecv.at[ci], sibling)
        acc[ci, qd] = acc[ci, qd] - trecv[ci].astype(F32)
        a_send[ci] = acc[ci].astype(BF16)
        send(r2_t[ci], a_send.at[ci], r2.at[ci], across)

    def residual(ci):
        arrived(r2_t[ci], r2.at[ci], across)
        errs[ci, c, pa, :, pb] = (acc[ci] + r2[ci].astype(F32)).astype(BF16)
        for k in range(1, INQ):
            send(e2_t[ci][k - 1], errs.at[ci, c, pa, :, pb], errs.at[ci, c, pa, :, pb], in_quad(k))

    def errors_pair(ci):
        for k in range(1, INQ):
            a, b = place(INQ - k)
            arrived(e2_t[ci][k - 1], errs.at[ci, c, a, :, b], in_quad(INQ - k))
        send(es_t[ci], errs.at[ci, c], errs.at[ci, c], sibling)

    def back(ci):
        arrived(es_t[ci], errs.at[ci, 1 - c], sibling)
        n = 0 if ci in (N1, F1) else 1
        for half in range(2):
            value = None
            for u in range(SECT):
                term = jnp.dot(
                    errs[ci, u, half].reshape(CHUNK // 2, HC), pt[u * HC : (u + 1) * HC, :],
                    preferred_element_type=F32,
                )
                value = term if value is None else value + term
            value = value.astype(BF16)
            if ci in NEAR:
                gnear[n, half] = value.reshape(NX, TOK, WS)
            else:
                gfar[n, 2 * half : 2 * half + 2] = value.reshape(2, 2, TOK, WS)
        for to, _, there, here in peers(ci):
            if ci in NEAR:
                send(gnear_t[here], gnear.at[n, to[0] % 2, to[1]], gnear_in.at[there], at(h, *to), gnear_t[0] + there)
            else:
                send(gfar_t[here], gfar.at[n, to[0], to[1] % 2], gfar_in.at[there], at(h, *to), gfar_t[0] + there)

    def collect(value, slots, sems, chunks):
        value = value.astype(F32)
        for ci in chunks:
            for _, of, _, here in peers(ci):
                arrived(sems[here], slots.at[here], at(h, *of))
                value = value + slots[here].astype(F32)
        return value

    def turn(ci):
        ft[ci] = rows_of(ci).T

    done = []

    def grad(ci):
        for u in range(SECT):
            term = jnp.dot(ft[ci], errs[ci, u].reshape(CHUNK, HC), preferred_element_type=F32)
            cols = slice(u * HC, (u + 1) * HC)
            if done:
                term = pgrad[:, cols] + term
            pgrad[:, cols] = term * (1.0 / math.sqrt(TOKENS)) if len(done) == 3 else term
        done.append(ci)

    def send_far():
        zsend[...] = collect(gfar[0, y, xb], gfar_in, gfar_t, (F1, F2)).astype(BF16)
        send(z_t, zsend, zrecv, z_mate)

    store_pgrad = pltpu.make_async_copy(pgrad, pgrad_hbm, load_sems.at[5])
    store_igrad = pltpu.make_async_copy(igrad, igrad_hbm, load_sems.at[6])

    far_in()
    predict(N1)
    send_teacher(jnp.logical_not(first_chunk))
    predict(N2)
    sum_pair(N1)
    predict(F1)
    sum_pair(N2)
    turn(N2)
    sum_pair(F1)
    predict(F2)
    sum_quad(N1)
    sum_pair(F2)
    sum_quad(F1)
    sum_quad(F2)
    turn(F1)
    turn(F2)
    residual(F1)
    sum_quad(N2)
    residual(F2)
    errors_pair(F1)
    residual(N1)
    back(F1)
    errors_pair(F2)
    grad(F1)
    residual(N2)
    back(F2)
    errors_pair(N1)
    errors_pair(N2)
    turn(N1)
    back(N1)
    grad(N1)
    send_far()
    back(N2)
    grad(F2)
    grad(N2)
    store_pgrad.start()
    sent.extend(rows_out)

    for op in sent:
        op.wait_send()
    sent.clear()

    feature_grad = collect(gnear[0, yb, x], gnear_in, gnear_t, (N1, N2))
    arrived(z_t, zrecv, z_mate)
    feature_grad = feature_grad + zrecv[...].astype(F32)
    upstream = feature_grad * sg_row

    inner = jnp.sum(upstream * unit, axis=1, keepdims=True)
    stat2[st] = jnp.sum(jnp.where(lanes == rows, inner, zero), axis=0, keepdims=True)
    inner_mean = column(exchange(stat2)(), 0) / DS
    igrad[...] = inv_s * (upstream - unit * inner_mean)
    store_igrad.start()

    for op in sent:
        op.wait_send()
    store_pgrad.wait()
    store_igrad.wait()
    assert used[0] <= SEMS, used


def store(pgrad_in, igrad_in, pgrad_out, igrad_out, pgrad, igrad, sems):
    step = WS // STORES
    hops = [(igrad_in, igrad, igrad_out)]
    for i in range(STORES):
        rows = pl.ds(i * step, step)
        hops.append((pgrad_in.at[rows], pgrad.at[rows], pgrad_out.at[rows]))
    into = [pltpu.make_async_copy(a, b, sems.at[0, i]) for i, (a, b, _) in enumerate(hops)]
    out = [pltpu.make_async_copy(b, c, sems.at[1, i]) for i, (_, b, c) in enumerate(hops)]
    for op in into:
        op.start()
    for first, second in zip(into, out):
        first.wait()
        second.start()
    for op in out:
        op.wait()


def body(teacher_rows, student_rows, projector, teacher_gain, student_gain):
    anywhere = pl.BlockSpec(memory_space=pl.ANY)
    piece = (2, 2, 2, TOK, HC)
    results = pl.pallas_call(
        kernel,
        out_shape=(
            jax.ShapeDtypeStruct((WS, WC), F32),
            jax.ShapeDtypeStruct((TOK, WS), F32),
        ),
        in_specs=[anywhere] * 5,
        out_specs=(anywhere, anywhere),
        scratch_shapes=[
            pltpu.VMEM((WS, WC), F32),
            pltpu.VMEM((TOK, WS), F32),
            pltpu.VMEM((WC, WS), BF16),
            pltpu.VMEM((4, WS, CHUNK), BF16),
            pltpu.VMEM((TOK, WT), BF16),
            pltpu.VMEM((TOK, WS), BF16),
            pltpu.VMEM((WS, WC), BF16),
            pltpu.VMEM((ST, WT // LANES, LANES), F32),
            pltpu.VMEM((ST, WS // LANES, LANES), F32),
            pltpu.VMEM((ST, 1, LANES), F32),
            pltpu.VMEM((ST, 1, LANES), F32),
            pltpu.VMEM((1, LANES), F32),
            pltpu.VMEM((1, LANES), F32),
            pltpu.VMEM((TOK, WS), BF16),
            pltpu.VMEM((NZH, NY, NX, TOK, WS), BF16),
            pltpu.VMEM((2, SECT, TOK, HC), BF16),
            pltpu.VMEM((4, TOK, HC), BF16),
            pltpu.VMEM((4, SECT) + piece, F32),
            pltpu.VMEM((4,) + piece, F32),
            pltpu.VMEM((4,) + piece, BF16),
            pltpu.VMEM((4, INQ - 1, QUADS, TOK, HC), BF16),
            pltpu.VMEM((4, QUADS, TOK, HC), F32),
            pltpu.VMEM((4, QUADS, TOK, HC), BF16),
            pltpu.VMEM((4, QUADS, TOK, HC), BF16),
            pltpu.VMEM((4, SECT) + piece, BF16),
            pltpu.VMEM((2, 2, NX, TOK, WS), BF16),
            pltpu.VMEM((2, NY, 2, TOK, WS), BF16),
            pltpu.VMEM((15, TOK, WS), BF16),
            pltpu.VMEM((15, TOK, WS), BF16),
            pltpu.VMEM((TOK, WS), BF16),
            pltpu.VMEM((TOK, WS), BF16),
            pltpu.SemaphoreType.DMA((7,)),
            pltpu.SemaphoreType.DMA((SEMS,)),
            pltpu.SemaphoreType.DMA((SEMS,)),
        ],
        compiler_params=pltpu.CompilerParams(
            collective_id=0, has_side_effects=True, vmem_limit_bytes=56 * 1024 * 1024
        ),
    )(
        teacher_rows,
        student_rows,
        projector,
        teacher_gain.reshape(ST, WT // LANES, LANES),
        student_gain.reshape(ST, WS // LANES, LANES),
    )
    return pl.pallas_call(
        store,
        out_shape=(
            jax.ShapeDtypeStruct((WS, WC), F32),
            jax.ShapeDtypeStruct((TOK, WS), F32),
        ),
        in_specs=[anywhere] * 2,
        out_specs=(anywhere, anywhere),
        scratch_shapes=[
            pltpu.VMEM((WS, WC), F32),
            pltpu.VMEM((TOK, WS), F32),
            pltpu.SemaphoreType.DMA((2, STORES + 1)),
        ],
        compiler_params=pltpu.CompilerParams(vmem_limit_bytes=60 * 1024 * 1024),
    )(*results)


def solution(mesh):
    return jax.shard_map(
        body,
        mesh=mesh,
        in_specs=(
            P("dp", ("sect", "tensor")),
            P("dp", ("sect", "tensor")),
            P(("sect", "tensor"), "dp"),
            P(),
            P(),
        ),
        out_specs=(P(("sect", "tensor"), "dp"), P("dp", ("sect", "tensor"))),
        check_vma=False,
    )
```

```python
import math

import jax
import jax.numpy as jnp
from jax import lax
from jax.experimental import pallas as pl
from jax.experimental.pallas import tpu as pltpu
from jax.sharding import PartitionSpec as P

epsilon = 1e-05

MESH = pl.DeviceIdType.MESH
DT = 16384
DS = 8192
TOKENS = 1024
SECT = 2
NX = 4
NY = 4
NZH = 2
DP = NZH * NY * NX
QUADS = 2
INQ = 4
TENSOR = QUADS * INQ
ST = SECT * TENSOR
TOK = TOKENS // DP
WT = DT // ST
WS = DS // ST
WC = DT // DP
HC = WC // SECT
CHUNK = TENSOR * TOK
LANES = 128
SEMS = 144
STORES = 4
F32 = jnp.float32
BF16 = jnp.bfloat16

N1, F1, F2, N2 = range(4)
NEAR = (N1, N2)


def kernel(
    teacher_hbm, student_hbm, proj_hbm, tgain_hbm, sgain_hbm,
    pgrad_hbm, igrad_hbm,
    pgrad, igrad, pt, ft, teacher, student, proj, tgain, sgain,
    stat, stat2, total_send, total_far, raw_far, feats, tsend, trecv, part, give, yrecv, ssend, r1, acc, a_send, r2,
    errs, gnear, gfar, gnear_in, gfar_in, zsend, zrecv,
    load_sems, send_sems, recv_sems,
):
    c = lax.axis_index("sect")
    d = lax.axis_index("dp")
    t = lax.axis_index("tensor")
    h, y, x = d // (NY * NX), (d // NX) % NY, d % NX
    qd, zi = t // INQ, t % INQ
    pa, pb = 1 - zi // 2, zi % 2
    st = c * TENSOR + t
    far = 1 - h
    yp, yb, xp, xb = y // 2, y % 2, x // 2, x % 2

    used = [0]
    sent = []

    def tickets(count):
        used[0] += count
        return range(used[0] - count, used[0])

    def dev(sect=None, dp=None, tensor=None):
        return {
            "sect": c if sect is None else sect,
            "dp": d if dp is None else dp,
            "tensor": t if tensor is None else tensor,
        }

    def send(i, src, dst, to, recv=None):
        op = pltpu.make_async_remote_copy(
            src_ref=src, dst_ref=dst, send_sem=send_sems.at[i],
            recv_sem=recv_sems.at[i if recv is None else recv],
            device_id=to, device_id_type=MESH,
        )
        op.start()
        sent.append(op)

    def arrived(i, dst, to):
        pltpu.make_async_remote_copy(
            src_ref=dst, dst_ref=dst, send_sem=send_sems.at[i], recv_sem=recv_sems.at[i],
            device_id=to, device_id_type=MESH,
        ).wait_recv()

    def at(zh, yy, xx):
        return dev(dp=zh * (NY * NX) + yy * NX + xx)

    def x_plus(k):
        return (x + k) % NX

    def y_plus(k):
        return (y + k) % NY

    y_mate, x_mate = y + 1 - 2 * yb, x + 1 - 2 * xb
    z_mate = at(far, y, x)
    sibling = dev(sect=1 - c)
    across = dev(tensor=(1 - qd) * INQ + zi)

    def peers(ci):
        first, out = ci in (N1, F1), []
        for r in range(2):
            for k in range(4):
                if first and r == 0 and k == 0:
                    continue
                if ci in NEAR:
                    line = (y, y_mate)[r] if first else 2 * (1 - yp) + r
                    to, of, mine = (line, x_plus(k)), (line, x_plus(NX - k)), yb
                else:
                    line = (x, x_mate)[r] if first else 2 * (1 - xp) + r
                    to, of, mine = (y_plus(k), line), (y_plus(NY - k), line), xb
                here = 4 * r + k - 1 if first else 7 + 4 * r + k
                there = here if first else 7 + 4 * mine + k
                out.append((to, of, there, here))
        return out

    def in_quad(k):
        return dev(tensor=qd * INQ + (zi + k) % INQ)

    def place(k):
        other = (zi + k) % INQ
        return 1 - other // 2, other % 2

    def st_dev(k):
        other = (st + k) % ST
        return other, dev(sect=other // TENSOR, tensor=other % TENSOR)

    loads = [
        pltpu.make_async_copy(src, dst, load_sems.at[i])
        for i, (src, dst) in enumerate(
            ((student_hbm, student), (teacher_hbm, teacher), (sgain_hbm, sgain), (tgain_hbm, tgain), (proj_hbm, proj))
        )
    ]
    for op in loads:
        op.start()

    barrier = pltpu.get_barrier_semaphore()

    def hello(to):
        pl.semaphore_signal(barrier, inc=1, device_id=to, device_id_type=MESH)

    for k in range(1, ST):
        hello(st_dev(k)[1])
    for k in range(1, NY * NX):
        hello(at(h, y_plus(k // NX), x_plus(k % NX)))
    hello(z_mate)
    source = dict(sect=(d // 2) // TENSOR, tensor=(d // 2) % TENSOR)
    for zh, yy, xx in (
        (h, 2 * yp + pa, 2 * qd + pb),
        (far, 2 * pa + qd, 2 * xp + pb),
        (far, 2 * pa + qd, 2 * (1 - xp) + pb),
        (h, 2 * (1 - yp) + pa, 2 * qd + pb),
    ):
        hello(dev(dp=zh * (NY * NX) + yy * NX + xx, **source))

    rows = lax.broadcasted_iota(jnp.int32, (TOK, LANES), 0)
    lanes = lax.broadcasted_iota(jnp.int32, (TOK, LANES), 1)
    zero = jnp.zeros((TOK, LANES), F32)

    def column(row, first):
        return jnp.sum(jnp.where(lanes == rows + first, row, zero), axis=1, keepdims=True)

    loads[0].wait()
    sf = student[...].astype(F32)
    ssum = jnp.sum(sf * sf, axis=1, keepdims=True)
    loads[1].wait()
    tf = teacher[...].astype(F32)
    tsum = jnp.sum(tf * tf, axis=1, keepdims=True)
    spread = jnp.where(lanes == rows, tsum, zero) + jnp.where(lanes == rows + TOK, ssum, zero)
    stat[st] = jnp.sum(spread, axis=0, keepdims=True)

    pl.semaphore_wait(barrier, (ST - 1) + (NY * NX - 1) + 1 + 4)

    def exchange(ref):
        own = tickets(ST - 1)
        for k in range(1, ST):
            send(own[k - 1], ref.at[st], ref.at[st], st_dev(k)[1])

        def finish():
            for k in range(1, ST):
                other, where = st_dev(ST - k)
                arrived(own[k - 1], ref.at[other], where)
            return jnp.sum(ref[...], axis=0)

        return finish

    finish_stat = exchange(stat)
    raw_t, total_t = tickets(2)
    send(raw_t, student, raw_far, z_mate)

    loads[2].wait()
    sg = sgain[st]
    sg_row = jnp.concatenate([sg[k : k + 1, :] for k in range(WS // LANES)], axis=1)
    loads[3].wait()
    tg = tgain[st]

    loads[4].wait()
    pt[...] = proj[...].T

    total = finish_stat()
    total_send[...] = total
    send(total_t, total_send, total_far, z_mate)
    inv_s = lax.rsqrt(column(total, TOK) / DS + epsilon)
    unit = sf * inv_s
    feats[h, y, x] = (unit * sg_row).astype(BF16)
    near_t, far_t = tickets(15), tickets(15)

    def spread(ci):
        zh, base = (h, near_t[0]) if ci in NEAR else (far, far_t[0])
        for to, _, there, here in peers(ci):
            send(base + here, feats.at[zh, y, x], feats.at[zh, y, x], at(h, *to), base + there)

    spread(N1)
    spread(N2)

    inv_t = lax.rsqrt(column(total, 0) / DT + epsilon)
    for k in range(WT // LANES):
        col = k * LANES
        value = tf[:, col : col + LANES] * inv_t * tg[k : k + 1, :]
        tsend[col // WC, (col % WC) // HC, :, col % HC : col % HC + LANES] = value.astype(BF16)

    tt = tickets(4)
    ts = tickets(4)
    rows_out = []
    near_there = h == c
    to_a = jnp.where(near_there, yb, yp)
    to_q = jnp.where(near_there, xp, yb)
    for j in range(2):
        xp_there = ((2 * t + j) % NX) // 2
        yp_there = t // INQ
        slot = jnp.where(
            near_there,
            jnp.where(yp == yp_there, N1, N2),
            jnp.where(xp == xp_there, F1, F2),
        )
        for u in range(SECT):
            rows_out.append(
                pltpu.make_async_remote_copy(
                    src_ref=tsend.at[j, u], dst_ref=trecv.at[slot],
                    send_sem=send_sems.at[ts[2 * j + u]], recv_sem=recv_sems.at[tt[0] + slot],
                    device_id=dev(sect=u, dp=2 * st + j, tensor=to_q * INQ + (1 - to_a) * 2 + xb),
                    device_id_type=MESH,
                )
            )

    first_chunk = jnp.logical_and(near_there, yp == t // INQ)

    def send_teacher(now):
        @pl.when(now)
        def _():
            for op in rows_out:
                op.start()

    send_teacher(first_chunk)

    def far_in():
        arrived(raw_t, raw_far, z_mate)
        arrived(total_t, total_far, z_mate)
        inv_far = lax.rsqrt(column(total_far[...], TOK) / DS + epsilon)
        feats[far, y, x] = (raw_far[...].astype(F32) * inv_far * sg_row).astype(BF16)
        spread(F1)
        spread(F2)

    def rows_of(ci):
        if ci in NEAR:
            return feats[h, pl.ds(2 * (yp if ci == N1 else 1 - yp), 2)].reshape(CHUNK, WS)
        return feats[far, :, pl.ds(2 * (xp if ci == F1 else 1 - xp), 2)].reshape(CHUNK, WS)

    def features_ready(ci):
        zh, base = (h, near_t[0]) if ci in NEAR else (far, far_t[0])
        for _, of, _, here in peers(ci):
            arrived(base + here, feats.at[zh, of[0], of[1]], at(h, *of))

    pair_t, r1_t, r2_t = tickets(4), [tickets(INQ - 1) for _ in range(4)], tickets(4)
    e2_t, es_t = [tickets(INQ - 1) for _ in range(4)], tickets(4)
    gnear_t, gfar_t = tickets(15), tickets(15)
    (z_t,) = tickets(1)

    def predict(ci):
        features_ready(ci)
        value = rows_of(ci)
        for theirs in (True, False):
            u = 1 - c if theirs else c
            half = jnp.dot(value, proj[:, pl.ds(pl.multiple_of(u * HC, HC), HC)], preferred_element_type=F32)
            half = half.reshape(2, 2, 2, TOK, HC)
            if theirs:
                give[ci] = half.astype(BF16)
                send(pair_t[ci], give.at[ci], yrecv.at[ci], sibling)
            else:
                part[ci] = half

    def sum_pair(ci):
        arrived(pair_t[ci], yrecv.at[ci], sibling)
        for k in range(1, INQ):
            a, b = place(k)
            ssend[ci, a, :, b] = (part[ci, a, :, b] + yrecv[ci, a, :, b].astype(F32)).astype(BF16)
            send(r1_t[ci][k - 1], ssend.at[ci, a, :, b], r1.at[ci, k - 1], in_quad(k))
        acc[ci] = part[ci, pa, :, pb] + yrecv[ci, pa, :, pb].astype(F32)

    def sum_quad(ci):
        value = acc[ci]
        for k in range(1, INQ):
            arrived(r1_t[ci][k - 1], r1.at[ci, k - 1], in_quad(INQ - k))
            value = value + r1[ci, k - 1].astype(F32)
        acc[ci] = value
        arrived(tt[ci], trecv.at[ci], sibling)
        acc[ci, qd] = acc[ci, qd] - trecv[ci].astype(F32)
        a_send[ci] = acc[ci].astype(BF16)
        send(r2_t[ci], a_send.at[ci], r2.at[ci], across)

    def residual(ci):
        arrived(r2_t[ci], r2.at[ci], across)
        errs[ci, c, pa, :, pb] = (acc[ci] + r2[ci].astype(F32)).astype(BF16)
        for k in range(1, INQ):
            send(e2_t[ci][k - 1], errs.at[ci, c, pa, :, pb], errs.at[ci, c, pa, :, pb], in_quad(k))

    def errors_pair(ci):
        for k in range(1, INQ):
            a, b = place(INQ - k)
            arrived(e2_t[ci][k - 1], errs.at[ci, c, a, :, b], in_quad(INQ - k))
        send(es_t[ci], errs.at[ci, c], errs.at[ci, c], sibling)

    def back(ci):
        arrived(es_t[ci], errs.at[ci, 1 - c], sibling)
        n = 0 if ci in (N1, F1) else 1
        for half in range(2):
            value = None
            for u in range(SECT):
                term = jnp.dot(
                    errs[ci, u, half].reshape(CHUNK // 2, HC), pt[u * HC : (u + 1) * HC, :],
                    preferred_element_type=F32,
                )
                value = term if value is None else value + term
            value = value.astype(BF16)
            if ci in NEAR:
                gnear[n, half] = value.reshape(NX, TOK, WS)
            else:
                gfar[n, 2 * half : 2 * half + 2] = value.reshape(2, 2, TOK, WS)
        for to, _, there, here in peers(ci):
            if ci in NEAR:
                send(gnear_t[here], gnear.at[n, to[0] % 2, to[1]], gnear_in.at[there], at(h, *to), gnear_t[0] + there)
            else:
                send(gfar_t[here], gfar.at[n, to[0], to[1] % 2], gfar_in.at[there], at(h, *to), gfar_t[0] + there)

    def collect(value, slots, sems, chunks):
        value = value.astype(F32)
        for ci in chunks:
            for _, of, _, here in peers(ci):
                arrived(sems[here], slots.at[here], at(h, *of))
                value = value + slots[here].astype(F32)
        return value

    def turn(ci):
        ft[ci] = rows_of(ci).T

    done = []

    def grad(ci):
        for u in range(SECT):
            term = jnp.dot(ft[ci], errs[ci, u].reshape(CHUNK, HC), preferred_element_type=F32)
            cols = slice(u * HC, (u + 1) * HC)
            if done:
                term = pgrad[:, cols] + term
            pgrad[:, cols] = term * (1.0 / math.sqrt(TOKENS)) if len(done) == 3 else term
        done.append(ci)

    def send_far():
        zsend[...] = collect(gfar[0, y, xb], gfar_in, gfar_t, (F1, F2)).astype(BF16)
        send(z_t, zsend, zrecv, z_mate)

    store_pgrad = pltpu.make_async_copy(pgrad, pgrad_hbm, load_sems.at[5])
    store_igrad = pltpu.make_async_copy(igrad, igrad_hbm, load_sems.at[6])

    far_in()
    predict(N1)
    send_teacher(jnp.logical_not(first_chunk))
    predict(N2)
    turn(N1)
    sum_pair(N1)
    predict(F1)
    sum_pair(N2)
    turn(N2)
    sum_pair(F1)
    predict(F2)
    sum_quad(N1)
    sum_pair(F2)
    sum_quad(F1)
    sum_quad(F2)
    turn(F1)
    turn(F2)
    residual(F1)
    sum_quad(N2)
    residual(F2)
    errors_pair(F1)
    residual(N1)
    back(F1)
    errors_pair(F2)
    grad(F1)
    residual(N2)
    back(F2)
    errors_pair(N1)
    errors_pair(N2)
    back(N1)
    send_far()
    back(N2)
    grad(N1)
    grad(F2)
    grad(N2)
    store_pgrad.start()
    sent.extend(rows_out)

    feature_grad = collect(gnear[0, yb, x], gnear_in, gnear_t, (N1, N2))
    arrived(z_t, zrecv, z_mate)
    feature_grad = feature_grad + zrecv[...].astype(F32)
    upstream = feature_grad * sg_row

    inner = jnp.sum(upstream * unit, axis=1, keepdims=True)
    stat2[st] = jnp.sum(jnp.where(lanes == rows, inner, zero), axis=0, keepdims=True)
    finish_stat2 = exchange(stat2)
    for op in sent:
        op.wait_send()
    inner_mean = column(finish_stat2(), 0) / DS
    igrad[...] = inv_s * (upstream - unit * inner_mean)
    store_igrad.start()
    store_pgrad.wait()
    store_igrad.wait()
    assert used[0] <= SEMS, used


def store(pgrad_in, igrad_in, pgrad_out, igrad_out, pgrad, igrad, sems):
    step = WS // STORES
    hops = [(igrad_in, igrad, igrad_out)]
    for i in range(STORES):
        rows = pl.ds(i * step, step)
        hops.append((pgrad_in.at[rows], pgrad.at[rows], pgrad_out.at[rows]))
    into = [pltpu.make_async_copy(a, b, sems.at[0, i]) for i, (a, b, _) in enumerate(hops)]
    out = [pltpu.make_async_copy(b, c, sems.at[1, i]) for i, (_, b, c) in enumerate(hops)]
    for op in into:
        op.start()
    for first, second in zip(into, out):
        first.wait()
        second.start()
    for op in out:
        op.wait()


def body(teacher_rows, student_rows, projector, teacher_gain, student_gain):
    anywhere = pl.BlockSpec(memory_space=pl.ANY)
    piece = (2, 2, 2, TOK, HC)
    results = pl.pallas_call(
        kernel,
        out_shape=(
            jax.ShapeDtypeStruct((WS, WC), F32),
            jax.ShapeDtypeStruct((TOK, WS), F32),
        ),
        in_specs=[anywhere] * 5,
        out_specs=(anywhere, anywhere),
        scratch_shapes=[
            pltpu.VMEM((WS, WC), F32),
            pltpu.VMEM((TOK, WS), F32),
            pltpu.VMEM((WC, WS), BF16),
            pltpu.VMEM((4, WS, CHUNK), BF16),
            pltpu.VMEM((TOK, WT), BF16),
            pltpu.VMEM((TOK, WS), BF16),
            pltpu.VMEM((WS, WC), BF16),
            pltpu.VMEM((ST, WT // LANES, LANES), F32),
            pltpu.VMEM((ST, WS // LANES, LANES), F32),
            pltpu.VMEM((ST, 1, LANES), F32),
            pltpu.VMEM((ST, 1, LANES), F32),
            pltpu.VMEM((1, LANES), F32),
            pltpu.VMEM((1, LANES), F32),
            pltpu.VMEM((TOK, WS), BF16),
            pltpu.VMEM((NZH, NY, NX, TOK, WS), BF16),
            pltpu.VMEM((2, SECT, TOK, HC), BF16),
            pltpu.VMEM((4, TOK, HC), BF16),
            pltpu.VMEM((4,) + piece, F32),
            pltpu.VMEM((4,) + piece, BF16),
            pltpu.VMEM((4,) + piece, BF16),
            pltpu.VMEM((4,) + piece, BF16),
            pltpu.VMEM((4, INQ - 1, QUADS, TOK, HC), BF16),
            pltpu.VMEM((4, QUADS, TOK, HC), F32),
            pltpu.VMEM((4, QUADS, TOK, HC), BF16),
            pltpu.VMEM((4, QUADS, TOK, HC), BF16),
            pltpu.VMEM((4, SECT) + piece, BF16),
            pltpu.VMEM((2, 2, NX, TOK, WS), BF16),
            pltpu.VMEM((2, NY, 2, TOK, WS), BF16),
            pltpu.VMEM((15, TOK, WS), BF16),
            pltpu.VMEM((15, TOK, WS), BF16),
            pltpu.VMEM((TOK, WS), BF16),
            pltpu.VMEM((TOK, WS), BF16),
            pltpu.SemaphoreType.DMA((7,)),
            pltpu.SemaphoreType.DMA((SEMS,)),
            pltpu.SemaphoreType.DMA((SEMS,)),
        ],
        compiler_params=pltpu.CompilerParams(
            collective_id=0, has_side_effects=True, vmem_limit_bytes=56 * 1024 * 1024
        ),
    )(
        teacher_rows,
        student_rows,
        projector,
        teacher_gain.reshape(ST, WT // LANES, LANES),
        student_gain.reshape(ST, WS // LANES, LANES),
    )
    return pl.pallas_call(
        store,
        out_shape=(
            jax.ShapeDtypeStruct((WS, WC), F32),
            jax.ShapeDtypeStruct((TOK, WS), F32),
        ),
        in_specs=[anywhere] * 2,
        out_specs=(anywhere, anywhere),
        scratch_shapes=[
            pltpu.VMEM((WS, WC), F32),
            pltpu.VMEM((TOK, WS), F32),
            pltpu.SemaphoreType.DMA((2, STORES + 1)),
        ],
        compiler_params=pltpu.CompilerParams(vmem_limit_bytes=60 * 1024 * 1024),
    )(*results)


def solution(mesh):
    return jax.shard_map(
        body,
        mesh=mesh,
        in_specs=(
            P("dp", ("sect", "tensor")),
            P("dp", ("sect", "tensor")),
            P(("sect", "tensor"), "dp"),
            P(),
            P(),
        ),
        out_specs=(P(("sect", "tensor"), "dp"), P("dp", ("sect", "tensor"))),
        check_vma=False,
    )
```

```python
import math

import jax
import jax.numpy as jnp
from jax import lax
from jax.experimental import pallas as pl
from jax.experimental.pallas import tpu as pltpu
from jax.sharding import PartitionSpec as P

epsilon = 1e-05

MESH = pl.DeviceIdType.MESH
DT = 16384
DS = 8192
TOKENS = 1024
SECT = 2
NX = 4
NY = 4
NZH = 2
DP = NZH * NY * NX
QUADS = 2
INQ = 4
TENSOR = QUADS * INQ
ST = SECT * TENSOR
TOK = TOKENS // DP
WT = DT // ST
WS = DS // ST
WC = DT // DP
HC = WC // SECT
CHUNK = TENSOR * TOK
LANES = 128
SEMS = 144
STORES = 4
F32 = jnp.float32
BF16 = jnp.bfloat16

N1, F1, F2, N2 = range(4)
NEAR = (N1, N2)


def kernel(
    teacher_hbm, student_hbm, proj_hbm, tgain_hbm, sgain_hbm,
    pgrad_hbm, igrad_hbm,
    pgrad, igrad, pt, ft, teacher, student, proj, tgain, sgain,
    stat, stat2, total_send, total_far, raw_far, feats, tsend, trecv, part, yrecv, ssend, r1, acc, a_send, r2,
    errs, gnear, gfar, gnear_in, gfar_in, zsend, zrecv,
    load_sems, send_sems, recv_sems,
):
    c = lax.axis_index("sect")
    d = lax.axis_index("dp")
    t = lax.axis_index("tensor")
    h, y, x = d // (NY * NX), (d // NX) % NY, d % NX
    qd, zi = t // INQ, t % INQ
    pa, pb = 1 - zi // 2, zi % 2
    st = c * TENSOR + t
    far = 1 - h
    yp, yb, xp, xb = y // 2, y % 2, x // 2, x % 2

    used = [0]
    sent = []

    def tickets(count):
        used[0] += count
        return range(used[0] - count, used[0])

    def dev(sect=None, dp=None, tensor=None):
        return {
            "sect": c if sect is None else sect,
            "dp": d if dp is None else dp,
            "tensor": t if tensor is None else tensor,
        }

    def send(i, src, dst, to, recv=None):
        op = pltpu.make_async_remote_copy(
            src_ref=src, dst_ref=dst, send_sem=send_sems.at[i],
            recv_sem=recv_sems.at[i if recv is None else recv],
            device_id=to, device_id_type=MESH,
        )
        op.start()
        sent.append(op)

    def arrived(i, dst, to):
        pltpu.make_async_remote_copy(
            src_ref=dst, dst_ref=dst, send_sem=send_sems.at[i], recv_sem=recv_sems.at[i],
            device_id=to, device_id_type=MESH,
        ).wait_recv()

    def at(zh, yy, xx):
        return dev(dp=zh * (NY * NX) + yy * NX + xx)

    def x_plus(k):
        return (x + k) % NX

    def y_plus(k):
        return (y + k) % NY

    y_mate, x_mate = y + 1 - 2 * yb, x + 1 - 2 * xb
    z_mate = at(far, y, x)
    sibling = dev(sect=1 - c)
    across = dev(tensor=(1 - qd) * INQ + zi)

    def peers(ci):
        first, out = ci in (N1, F1), []
        for r in range(2):
            for k in range(4):
                if first and r == 0 and k == 0:
                    continue
                if ci in NEAR:
                    line = (y, y_mate)[r] if first else 2 * (1 - yp) + r
                    to, of, mine = (line, x_plus(k)), (line, x_plus(NX - k)), yb
                else:
                    line = (x, x_mate)[r] if first else 2 * (1 - xp) + r
                    to, of, mine = (y_plus(k), line), (y_plus(NY - k), line), xb
                here = 4 * r + k - 1 if first else 7 + 4 * r + k
                there = here if first else 7 + 4 * mine + k
                out.append((to, of, there, here))
        return out

    def in_quad(k):
        return dev(tensor=qd * INQ + (zi + k) % INQ)

    def place(k):
        other = (zi + k) % INQ
        return 1 - other // 2, other % 2

    def st_dev(k):
        other = (st + k) % ST
        return other, dev(sect=other // TENSOR, tensor=other % TENSOR)

    loads = [
        pltpu.make_async_copy(src, dst, load_sems.at[i])
        for i, (src, dst) in enumerate(
            ((student_hbm, student), (teacher_hbm, teacher), (sgain_hbm, sgain), (tgain_hbm, tgain), (proj_hbm, proj))
        )
    ]
    for op in loads:
        op.start()

    barrier = pltpu.get_barrier_semaphore()

    def hello(to):
        pl.semaphore_signal(barrier, inc=1, device_id=to, device_id_type=MESH)

    for k in range(1, ST):
        hello(st_dev(k)[1])
    for k in range(1, NY * NX):
        hello(at(h, y_plus(k // NX), x_plus(k % NX)))
    hello(z_mate)
    source = dict(sect=(d // 2) // TENSOR, tensor=(d // 2) % TENSOR)
    for zh, yy, xx in (
        (h, 2 * yp + pa, 2 * qd + pb),
        (far, 2 * pa + qd, 2 * xp + pb),
        (far, 2 * pa + qd, 2 * (1 - xp) + pb),
        (h, 2 * (1 - yp) + pa, 2 * qd + pb),
    ):
        hello(dev(dp=zh * (NY * NX) + yy * NX + xx, **source))

    rows = lax.broadcasted_iota(jnp.int32, (TOK, LANES), 0)
    lanes = lax.broadcasted_iota(jnp.int32, (TOK, LANES), 1)
    zero = jnp.zeros((TOK, LANES), F32)

    def column(row, first):
        return jnp.sum(jnp.where(lanes == rows + first, row, zero), axis=1, keepdims=True)

    loads[0].wait()
    sf = student[...].astype(F32)
    ssum = jnp.sum(sf * sf, axis=1, keepdims=True)
    loads[1].wait()
    tf = teacher[...].astype(F32)
    tsum = jnp.sum(tf * tf, axis=1, keepdims=True)
    spread = jnp.where(lanes == rows, tsum, zero) + jnp.where(lanes == rows + TOK, ssum, zero)
    stat[st] = jnp.sum(spread, axis=0, keepdims=True)

    pl.semaphore_wait(barrier, (ST - 1) + (NY * NX - 1) + 1 + 4)

    def exchange(ref):
        own = tickets(ST - 1)
        for k in range(1, ST):
            send(own[k - 1], ref.at[st], ref.at[st], st_dev(k)[1])

        def finish():
            for k in range(1, ST):
                other, where = st_dev(ST - k)
                arrived(own[k - 1], ref.at[other], where)
            return jnp.sum(ref[...], axis=0)

        return finish

    raw_t, total_t = tickets(2)
    send(raw_t, student, raw_far, z_mate)
    finish_stat = exchange(stat)

    loads[2].wait()
    sg = sgain[st]
    sg_row = jnp.concatenate([sg[k : k + 1, :] for k in range(WS // LANES)], axis=1)
    loads[3].wait()
    tg = tgain[st]

    loads[4].wait()
    pt[...] = proj[...].T

    total = finish_stat()
    total_send[...] = total
    send(total_t, total_send, total_far, z_mate)
    inv_s = lax.rsqrt(column(total, TOK) / DS + epsilon)
    unit = sf * inv_s
    feats[h, y, x] = (unit * sg_row).astype(BF16)
    near_t, far_t = tickets(15), tickets(15)

    def spread(ci):
        zh, base = (h, near_t[0]) if ci in NEAR else (far, far_t[0])
        for to, _, there, here in peers(ci):
            send(base + here, feats.at[zh, y, x], feats.at[zh, y, x], at(h, *to), base + there)

    spread(N1)
    spread(N2)

    inv_t = lax.rsqrt(column(total, 0) / DT + epsilon)
    for k in range(WT // LANES):
        col = k * LANES
        value = tf[:, col : col + LANES] * inv_t * tg[k : k + 1, :]
        tsend[col // WC, (col % WC) // HC, :, col % HC : col % HC + LANES] = value.astype(BF16)

    tt = tickets(4)
    ts = tickets(4)
    rows_out = []
    near_there = h == c
    to_a = jnp.where(near_there, yb, yp)
    to_q = jnp.where(near_there, xp, yb)
    for j in range(2):
        xp_there = ((2 * t + j) % NX) // 2
        yp_there = t // INQ
        slot = jnp.where(
            near_there,
            jnp.where(yp == yp_there, N1, N2),
            jnp.where(xp == xp_there, F1, F2),
        )
        for u in range(SECT):
            rows_out.append(
                pltpu.make_async_remote_copy(
                    src_ref=tsend.at[j, u], dst_ref=trecv.at[slot],
                    send_sem=send_sems.at[ts[2 * j + u]], recv_sem=recv_sems.at[tt[0] + slot],
                    device_id=dev(sect=u, dp=2 * st + j, tensor=to_q * INQ + (1 - to_a) * 2 + xb),
                    device_id_type=MESH,
                )
            )

    first_chunk = jnp.logical_and(near_there, yp == t // INQ)

    def send_teacher(now):
        @pl.when(now)
        def _():
            for op in rows_out:
                op.start()

    send_teacher(first_chunk)

    def far_in():
        arrived(raw_t, raw_far, z_mate)
        arrived(total_t, total_far, z_mate)
        inv_far = lax.rsqrt(column(total_far[...], TOK) / DS + epsilon)
        feats[far, y, x] = (raw_far[...].astype(F32) * inv_far * sg_row).astype(BF16)
        spread(F1)
        spread(F2)

    def rows_of(ci):
        if ci in NEAR:
            return feats[h, pl.ds(2 * (yp if ci == N1 else 1 - yp), 2)].reshape(CHUNK, WS)
        return feats[far, :, pl.ds(2 * (xp if ci == F1 else 1 - xp), 2)].reshape(CHUNK, WS)

    def features_ready(ci):
        zh, base = (h, near_t[0]) if ci in NEAR else (far, far_t[0])
        for _, of, _, here in peers(ci):
            arrived(base + here, feats.at[zh, of[0], of[1]], at(h, *of))

    pair_t, r1_t, r2_t = tickets(4), [tickets(INQ - 1) for _ in range(4)], tickets(4)
    e2_t, es_t = [tickets(INQ - 1) for _ in range(4)], tickets(4)
    gnear_t, gfar_t = tickets(15), tickets(15)
    (z_t,) = tickets(1)

    def predict(ci):
        features_ready(ci)
        value = rows_of(ci)
        for theirs in (True, False):
            u = 1 - c if theirs else c
            half = jnp.dot(value, proj[:, pl.ds(pl.multiple_of(u * HC, HC), HC)], preferred_element_type=F32)
            part[ci, u] = half.reshape(2, 2, 2, TOK, HC)
            if theirs:
                send(pair_t[ci], part.at[ci, u], yrecv.at[ci], sibling)

    def sum_pair(ci):
        arrived(pair_t[ci], yrecv.at[ci], sibling)
        for k in range(1, INQ):
            a, b = place(k)
            ssend[ci, a, :, b] = (part[ci, c, a, :, b] + yrecv[ci, a, :, b]).astype(BF16)
            send(r1_t[ci][k - 1], ssend.at[ci, a, :, b], r1.at[ci, k - 1], in_quad(k))
        acc[ci] = part[ci, c, pa, :, pb] + yrecv[ci, pa, :, pb]

    def sum_quad(ci):
        value = acc[ci]
        for k in range(1, INQ):
            arrived(r1_t[ci][k - 1], r1.at[ci, k - 1], in_quad(INQ - k))
            value = value + r1[ci, k - 1].astype(F32)
        acc[ci] = value
        arrived(tt[ci], trecv.at[ci], sibling)
        acc[ci, qd] = acc[ci, qd] - trecv[ci].astype(F32)
        a_send[ci] = acc[ci].astype(BF16)
        send(r2_t[ci], a_send.at[ci], r2.at[ci], across)

    def residual(ci):
        arrived(r2_t[ci], r2.at[ci], across)
        errs[ci, c, pa, :, pb] = (acc[ci] + r2[ci].astype(F32)).astype(BF16)
        for k in range(1, INQ):
            send(e2_t[ci][k - 1], errs.at[ci, c, pa, :, pb], errs.at[ci, c, pa, :, pb], in_quad(k))

    def errors_pair(ci):
        for k in range(1, INQ):
            a, b = place(INQ - k)
            arrived(e2_t[ci][k - 1], errs.at[ci, c, a, :, b], in_quad(INQ - k))
        send(es_t[ci], errs.at[ci, c], errs.at[ci, c], sibling)

    def back(ci):
        arrived(es_t[ci], errs.at[ci, 1 - c], sibling)
        n = 0 if ci in (N1, F1) else 1
        for half in range(2):
            value = None
            for u in range(SECT):
                term = jnp.dot(
                    errs[ci, u, half].reshape(CHUNK // 2, HC), pt[u * HC : (u + 1) * HC, :],
                    preferred_element_type=F32,
                )
                value = term if value is None else value + term
            value = value.astype(BF16)
            if ci in NEAR:
                gnear[n, half] = value.reshape(NX, TOK, WS)
            else:
                gfar[n, 2 * half : 2 * half + 2] = value.reshape(2, 2, TOK, WS)
        for to, _, there, here in peers(ci):
            if ci in NEAR:
                send(gnear_t[here], gnear.at[n, to[0] % 2, to[1]], gnear_in.at[there], at(h, *to), gnear_t[0] + there)
            else:
                send(gfar_t[here], gfar.at[n, to[0], to[1] % 2], gfar_in.at[there], at(h, *to), gfar_t[0] + there)

    def collect(value, slots, sems, chunks):
        value = value.astype(F32)
        for ci in chunks:
            for _, of, _, here in peers(ci):
                arrived(sems[here], slots.at[here], at(h, *of))
                value = value + slots[here].astype(F32)
        return value

    def turn(ci):
        ft[ci] = rows_of(ci).T

    done = []

    def grad(ci):
        for u in range(SECT):
            term = jnp.dot(ft[ci], errs[ci, u].reshape(CHUNK, HC), preferred_element_type=F32)
            cols = slice(u * HC, (u + 1) * HC)
            if done:
                term = pgrad[:, cols] + term
            pgrad[:, cols] = term * (1.0 / math.sqrt(TOKENS)) if len(done) == 3 else term
        done.append(ci)

    def send_far():
        zsend[...] = collect(gfar[0, y, xb], gfar_in, gfar_t, (F1, F2)).astype(BF16)
        send(z_t, zsend, zrecv, z_mate)

    store_pgrad = pltpu.make_async_copy(pgrad, pgrad_hbm, load_sems.at[5])
    store_igrad = pltpu.make_async_copy(igrad, igrad_hbm, load_sems.at[6])

    far_in()
    predict(N1)
    send_teacher(jnp.logical_not(first_chunk))
    predict(N2)
    sum_pair(N1)
    predict(F1)
    sum_pair(N2)
    turn(N2)
    sum_pair(F1)
    predict(F2)
    sum_quad(N1)
    sum_pair(F2)
    sum_quad(F1)
    sum_quad(F2)
    turn(F1)
    turn(F2)
    residual(F1)
    sum_quad(N2)
    residual(F2)
    errors_pair(F1)
    residual(N1)
    back(F1)
    errors_pair(F2)
    grad(F1)
    residual(N2)
    back(F2)
    errors_pair(N1)
    errors_pair(N2)
    turn(N1)
    back(N1)
    grad(N1)
    send_far()
    back(N2)
    grad(F2)
    grad(N2)
    store_pgrad.start()
    sent.extend(rows_out)

    for op in sent:
        op.wait_send()
    sent.clear()

    feature_grad = collect(gnear[0, yb, x], gnear_in, gnear_t, (N1, N2))
    arrived(z_t, zrecv, z_mate)
    feature_grad = feature_grad + zrecv[...].astype(F32)
    upstream = feature_grad * sg_row

    inner = jnp.sum(upstream * unit, axis=1, keepdims=True)
    stat2[st] = jnp.sum(jnp.where(lanes == rows, inner, zero), axis=0, keepdims=True)
    inner_mean = column(exchange(stat2)(), 0) / DS
    igrad[...] = inv_s * (upstream - unit * inner_mean)
    store_igrad.start()

    for op in sent:
        op.wait_send()
    store_pgrad.wait()
    store_igrad.wait()
    assert used[0] <= SEMS, used


def store(pgrad_in, igrad_in, pgrad_out, igrad_out, pgrad, igrad, sems):
    step = WS // STORES
    hops = [(igrad_in, igrad, igrad_out)]
    for i in range(STORES):
        rows = pl.ds(i * step, step)
        hops.append((pgrad_in.at[rows], pgrad.at[rows], pgrad_out.at[rows]))
    into = [pltpu.make_async_copy(a, b, sems.at[0, i]) for i, (a, b, _) in enumerate(hops)]
    out = [pltpu.make_async_copy(b, c, sems.at[1, i]) for i, (_, b, c) in enumerate(hops)]
    for op in into:
        op.start()
    for first, second in zip(into, out):
        first.wait()
        second.start()
    for op in out:
        op.wait()


def body(teacher_rows, student_rows, projector, teacher_gain, student_gain):
    anywhere = pl.BlockSpec(memory_space=pl.ANY)
    piece = (2, 2, 2, TOK, HC)
    results = pl.pallas_call(
        kernel,
        out_shape=(
            jax.ShapeDtypeStruct((WS, WC), F32),
            jax.ShapeDtypeStruct((TOK, WS), F32),
        ),
        in_specs=[anywhere] * 5,
        out_specs=(anywhere, anywhere),
        scratch_shapes=[
            pltpu.VMEM((WS, WC), F32),
            pltpu.VMEM((TOK, WS), F32),
            pltpu.VMEM((WC, WS), BF16),
            pltpu.VMEM((4, WS, CHUNK), BF16),
            pltpu.VMEM((TOK, WT), BF16),
            pltpu.VMEM((TOK, WS), BF16),
            pltpu.VMEM((WS, WC), BF16),
            pltpu.VMEM((ST, WT // LANES, LANES), F32),
            pltpu.VMEM((ST, WS // LANES, LANES), F32),
            pltpu.VMEM((ST, 1, LANES), F32),
            pltpu.VMEM((ST, 1, LANES), F32),
            pltpu.VMEM((1, LANES), F32),
            pltpu.VMEM((1, LANES), F32),
            pltpu.VMEM((TOK, WS), BF16),
            pltpu.VMEM((NZH, NY, NX, TOK, WS), BF16),
            pltpu.VMEM((2, SECT, TOK, HC), BF16),
            pltpu.VMEM((4, TOK, HC), BF16),
            pltpu.VMEM((4, SECT) + piece, F32),
            pltpu.VMEM((4,) + piece, F32),
            pltpu.VMEM((4,) + piece, BF16),
            pltpu.VMEM((4, INQ - 1, QUADS, TOK, HC), BF16),
            pltpu.VMEM((4, QUADS, TOK, HC), F32),
            pltpu.VMEM((4, QUADS, TOK, HC), BF16),
            pltpu.VMEM((4, QUADS, TOK, HC), BF16),
            pltpu.VMEM((4, SECT) + piece, BF16),
            pltpu.VMEM((2, 2, NX, TOK, WS), BF16),
            pltpu.VMEM((2, NY, 2, TOK, WS), BF16),
            pltpu.VMEM((15, TOK, WS), BF16),
            pltpu.VMEM((15, TOK, WS), BF16),
            pltpu.VMEM((TOK, WS), BF16),
            pltpu.VMEM((TOK, WS), BF16),
            pltpu.SemaphoreType.DMA((7,)),
            pltpu.SemaphoreType.DMA((SEMS,)),
            pltpu.SemaphoreType.DMA((SEMS,)),
        ],
        compiler_params=pltpu.CompilerParams(
            collective_id=0, has_side_effects=True, vmem_limit_bytes=56 * 1024 * 1024
        ),
    )(
        teacher_rows,
        student_rows,
        projector,
        teacher_gain.reshape(ST, WT // LANES, LANES),
        student_gain.reshape(ST, WS // LANES, LANES),
    )
    return pl.pallas_call(
        store,
        out_shape=(
            jax.ShapeDtypeStruct((WS, WC), F32),
            jax.ShapeDtypeStruct((TOK, WS), F32),
        ),
        in_specs=[anywhere] * 2,
        out_specs=(anywhere, anywhere),
        scratch_shapes=[
            pltpu.VMEM((WS, WC), F32),
            pltpu.VMEM((TOK, WS), F32),
            pltpu.SemaphoreType.DMA((2, STORES + 1)),
        ],
        compiler_params=pltpu.CompilerParams(vmem_limit_bytes=60 * 1024 * 1024),
    )(*results)


def solution(mesh):
    return jax.shard_map(
        body,
        mesh=mesh,
        in_specs=(
            P("dp", ("sect", "tensor")),
            P("dp", ("sect", "tensor")),
            P(("sect", "tensor"), "dp"),
            P(),
            P(),
        ),
        out_specs=(P(("sect", "tensor"), "dp"), P("dp", ("sect", "tensor"))),
        check_vma=False,
    )
```
